256 devices in a mesh: row: 16 (over x, z_lo), col: 16 (over y, z_hi, core).
Axes of the slice: x: 4, y: 4, z: 8 (z_hi: 2, z_lo: 4; z = z_hi * 4 + z_lo), core: 2. Of those that a mesh axis runs over, the one named last changes fastest.
Arguments:
- left_edges: bfloat16 [128, 256, 128], P('row', 'col'), may hold values from -6 to 6
- right_edges: bfloat16 [256, 256, 128], P('row', 'col'), may hold values from -6 to 6
- left_mask: int32 [128, 256], P('row', 'col'), may hold values 0 or 1
- right_mask: int32 [256, 256], P('row', 'col'), may hold values 0 or 1
- cotangent: bfloat16 [128, 256, 128], P('row', 'col'), may hold values from -6 to 6
- query_weight: bfloat16 [128, 128], replicated, may hold values from -1 to 1
- key_weight: bfloat16 [128, 128], replicated, may hold values from -1 to 1
- left_weight: bfloat16 [128, 128], replicated, may hold values from -0.5 to 0.5
- right_weight: bfloat16 [128, 128], replicated, may hold values from -0.5 to 0.5
- out_weight: bfloat16 [128, 128], replicated, may hold values from -0.5 to 0.5
Outputs:
- left_grad: float32 [128, 256, 128], P('row', 'col')
- right_grad: float32 [256, 256, 128], P('row', 'col')
- proj_grads: float32 [4, 128, 128], replicated
- out_grad: float32 [128, 128], replicated
The draws below stay inside these ranges and needn't reach their ends.
All inputs are finite; a program needn't handle non-finite values. No bound on the sum of `left_mask` or of `right_mask` on one device may be relied on, other than what follows from the above.
Results may differ from the reference program's by a relative error of at most 0.019.
The reference program's roundings to bfloat16 on the way count: a program that leaves them out, or rounds other values in their place, can miss the bound.
Values may be sent and summed in bfloat16 or wider, within the bound.
No kernel may reach another device: no remote copies, remote signals or barrier semaphores. Data moves between devices by JAX's collectives and lax.ppermute only.
A program may use at most 128 MiB of HBM per device.

```python
import math
import jax
import jax.numpy as jnp
from jax import lax

D = 128
HEADS = 4
HEAD_DIM = 32
NODES = 256
ROWS = 128
HIDDEN_WIDTH = 128


def draw_left_edges(key, part):
    key = jax.random.fold_in(key, 11)
    edges = jnp.clip(jax.random.normal(key, (ROWS, NODES, D), jnp.float32), -6.0, 6.0)
    return edges.astype(jnp.bfloat16)


def draw_right_edges(key, part):
    key = jax.random.fold_in(key, 12)
    edges = jnp.clip(jax.random.normal(key, (NODES, NODES, D), jnp.float32), -6.0, 6.0)
    return edges.astype(jnp.bfloat16)


def draw_query_weight(key, part):
    key = jax.random.fold_in(key, 13)
    matrix = jnp.clip(jax.random.normal(key, (D, HIDDEN_WIDTH), jnp.float32), -4.0, 4.0) * D ** (-0.5)
    return matrix.astype(jnp.bfloat16)


def draw_key_weight(key, part):
    key = jax.random.fold_in(key, 14)
    matrix = jnp.clip(jax.random.normal(key, (D, HIDDEN_WIDTH), jnp.float32), -4.0, 4.0) * D ** (-0.5)
    return matrix.astype(jnp.bfloat16)


def with_ends(values, key, least, largest):
    place = [jax.random.randint(jax.random.fold_in(key, axis), (), 0, length) for axis, length in enumerate(values.shape)]
    widest = values.shape.index(max(values.shape))
    neighbour = place[:widest] + [(place[widest] + 1) % values.shape[widest]] + place[widest + 1:]
    return values.at[tuple(place)].set(least).at[tuple(neighbour)].set(largest)


def steps_of(key, shape, cuts, low, high):
    def one(dim, blocks):
        steps = jax.random.uniform(jax.random.fold_in(jax.random.fold_in(key, 6), dim), (blocks,), jnp.float32, low / len(cuts), high / len(cuts))
        return jnp.repeat(jnp.exp(steps), shape[dim] // blocks).reshape((-1,) + (1,) * (len(shape) - dim - 1))

    loudness = one(*cuts[0])
    for cut in cuts[1:]:
        loudness = loudness * one(*cut)
    return loudness


def bell_draw(key, shape, scale, most, cuts=(), held_as=jnp.bfloat16):
    entries = jax.random.normal(key, shape, jnp.float32) * scale
    if len(cuts) > 0:
        entries = steps_of(key, shape, cuts, -0.22, 0.18) * entries
    return jnp.clip(entries, min=-most, max=most).astype(held_as)


def setup_inputs(seed: int = 0) -> dict:
    key_of = jax.random.split(jax.random.key(seed), 11)
    left_edges = draw_left_edges(jax.random.fold_in(key_of[10], 71), 0)
    right_edges = draw_right_edges(jax.random.fold_in(key_of[10], 71), 0)
    left_mask = with_ends((jax.random.randint(key_of[2], (ROWS, NODES), 0, 4) < 3).astype(jnp.int32), jax.random.fold_in(key_of[2], 1), 0, 1)
    right_mask = with_ends((jax.random.randint(key_of[3], (NODES, NODES), 0, 4) < 3).astype(jnp.int32), jax.random.fold_in(key_of[3], 1), 0, 1)
    cotangent = bell_draw(key_of[4], (ROWS, NODES, D), 1.0, 6.0, ((0, 16), (1, 16)))
    query_weight = draw_query_weight(jax.random.fold_in(key_of[10], 71), 0)
    key_weight = draw_key_weight(jax.random.fold_in(key_of[10], 71), 0)
    left_weight = bell_draw(key_of[7], (D, HIDDEN_WIDTH), D ** -0.5, 0.5)
    right_weight = bell_draw(key_of[8], (D, HIDDEN_WIDTH), D ** -0.5, 0.5)
    out_weight = bell_draw(key_of[9], (HIDDEN_WIDTH, D), HIDDEN_WIDTH ** -0.5, 0.5)
    return dict(left_edges=left_edges, right_edges=right_edges, left_mask=left_mask, right_mask=right_mask, cotangent=cotangent, query_weight=query_weight, key_weight=key_weight, left_weight=left_weight, right_weight=right_weight, out_weight=out_weight)


highest = lax.Precision.HIGHEST

def project(edges, weight):
    flat = edges.reshape(-1, edges.shape[-1])
    result = jnp.dot(flat, weight, preferred_element_type=jnp.float32).astype(jnp.bfloat16)
    result = lax.optimization_barrier(result)
    return result.reshape(edges.shape[:-1] + (weight.shape[1],))

def rounded(values):
    return lax.optimization_barrier(values.astype(jnp.bfloat16)).astype(jnp.float32)

def normalized(scores, allowed):
    scores = jnp.where(allowed, scores, -1000000000.0)
    highest_score = lax.optimization_barrier(jnp.max(scores, axis=1, keepdims=True))
    raw_weights = jnp.exp(scores - highest_score)
    return raw_weights / lax.optimization_barrier(jnp.sum(raw_weights, axis=1, keepdims=True))

def dense(data, weight):
    flat = data.reshape(-1, data.shape[-1])
    result = jnp.dot(flat, weight.astype(jnp.float32).T, precision=highest)
    return result.reshape(data.shape[:-1] + (weight.shape[0],))

def outer_sum(edges, grads):
    left_flat = edges.reshape(-1, edges.shape[-1]).astype(jnp.float32)
    return jnp.dot(left_flat.T, grads.reshape(-1, grads.shape[-1]), precision=highest)

def row_terms(query_row, left_row, mask_row, key_all, right_all, right_mask, upstream_row, scaling):
    scores = jnp.einsum('lhe,ljhe->jlh', query_row, key_all, precision=highest) * scaling
    allowed = (mask_row[None, :] * right_mask.T > 0)[:, :, None]
    weights = normalized(scores, allowed)
    weights_low = rounded(weights)
    value_out = jnp.einsum('jlh,lhe,ljhe->jhe', weights_low, left_row, right_all, precision=highest)
    weight_grad = jnp.einsum('jhe,lhe,ljhe->jlh', upstream_row, left_row, right_all, precision=highest)
    score_grad = rounded(weights * (weight_grad - lax.optimization_barrier(jnp.sum(weights * weight_grad, axis=1, keepdims=True))) * scaling)
    grad_query = jnp.einsum('jlh,ljhe->lhe', score_grad, key_all, precision=highest)
    grad_left = jnp.einsum('jlh,jhe,ljhe->lhe', weights_low, upstream_row, right_all, precision=highest)
    return (value_out.astype(jnp.bfloat16), grad_query, grad_left)

def column_terms(key_col, right_col, mask_col, query_all, left_all, left_mask, upstream_col, scaling):
    scores = jnp.einsum('ilhe,lhe->ilh', query_all, key_col, precision=highest) * scaling
    allowed = (left_mask * mask_col[None, :] > 0)[:, :, None]
    weights = normalized(scores, allowed)
    weights_low = rounded(weights)
    weight_grad = jnp.einsum('ihe,ilhe,lhe->ilh', upstream_col, left_all, right_col, precision=highest)
    score_grad = rounded(weights * (weight_grad - lax.optimization_barrier(jnp.sum(weights * weight_grad, axis=1, keepdims=True))) * scaling)
    grad_key = jnp.einsum('ilh,ilhe->lhe', score_grad, query_all, precision=highest)
    grad_right = jnp.einsum('ilh,ihe,ilhe->lhe', weights_low, upstream_col, left_all, precision=highest)
    return (grad_key, grad_right)

def reference(left_edges, right_edges, left_mask, right_mask, cotangent, query_weight, key_weight, left_weight, right_weight, out_weight):
    scaling = 1.0 / math.sqrt(HEAD_DIM)
    left_shape = (ROWS, NODES, HEADS, HEAD_DIM)
    right_shape = (NODES, NODES, HEADS, HEAD_DIM)
    query = project(left_edges, query_weight).astype(jnp.float32).reshape(left_shape)
    left_value = project(left_edges, left_weight).astype(jnp.float32).reshape(left_shape)
    key_all = project(right_edges, key_weight).astype(jnp.float32).reshape(right_shape)
    right_value = project(right_edges, right_weight).astype(jnp.float32).reshape(right_shape)
    upstream = rounded(jnp.dot(cotangent.reshape(-1, D), out_weight.T, preferred_element_type=jnp.float32)).reshape(left_shape)

    def along_rows(inputs):
        query_row, left_row, mask_row, upstream_row = inputs
        return row_terms(query_row, left_row, mask_row, key_all, right_value, right_mask, upstream_row, scaling)
    attended, grad_query, grad_left = lax.map(along_rows, (query, left_value, left_mask, upstream))

    def along_columns(inputs):
        key_col, right_col, mask_col, upstream_col = inputs
        return column_terms(key_col, right_col, mask_col, query, left_value, left_mask, upstream_col, scaling)
    key_cols, right_cols = lax.map(along_columns, (jnp.swapaxes(key_all, 0, 1), jnp.swapaxes(right_value, 0, 1), right_mask.T, jnp.swapaxes(upstream, 0, 1)))
    hidden_width = HEADS * HEAD_DIM
    grad_query = grad_query.reshape(ROWS, NODES, hidden_width)
    grad_left = grad_left.reshape(ROWS, NODES, hidden_width)
    key_sum = jnp.swapaxes(key_cols, 0, 1).reshape(NODES, NODES, hidden_width)
    right_sum = jnp.swapaxes(right_cols, 0, 1).reshape(NODES, NODES, hidden_width)
    left_grad = dense(grad_query, query_weight) + dense(grad_left, left_weight)
    right_grad = dense(key_sum, key_weight) + dense(right_sum, right_weight)
    proj_grads = jnp.stack([outer_sum(left_edges, grad_query), outer_sum(right_edges, key_sum), outer_sum(left_edges, grad_left), outer_sum(right_edges, right_sum)])
    out_grad = jnp.dot(attended.reshape(-1, hidden_width).T, cotangent.reshape(-1, D), preferred_element_type=jnp.float32)
    return (left_grad, right_grad, proj_grads, out_grad)
```

```python
import math

import jax
import jax.numpy as jnp
from jax import lax
from jax.sharding import PartitionSpec as P

HEADS = 4
HEAD_DIM = 32
BF = jnp.bfloat16
F32 = jnp.float32


def flip(k):
    return [(i, i ^ k) for i in range(16)]


def gather_col(block):
    pair = jnp.stack([block, lax.ppermute(block, "col", flip(2))])
    quads = jnp.concatenate([pair] + [lax.ppermute(pair, "col", flip(k)) for k in (4, 8, 12)])
    return jnp.concatenate([quads, lax.ppermute(quads, "col", flip(1))])


def gather_row(block):
    line = jnp.stack([block] + [lax.ppermute(block, "row", flip(k)) for k in (1, 2, 3)])
    return jnp.concatenate([line] + [lax.ppermute(line, "row", flip(k)) for k in (4, 8, 12)])


def left_place(col, b):
    apart = col ^ b
    return (apart & 1) * 8 + (apart >> 2) * 2 + ((apart >> 1) & 1)


def right_place(row, b):
    return row ^ b


def add_up(own, others):
    total = own.astype(F32)
    for other in others:
        total = total + other.astype(F32)
    return total


def meet(own, axis, flips):
    came = [lax.ppermute(own, axis, flip(k)).astype(F32) for k in flips]
    return (own.astype(F32) + came[0]) + (came[1] + came[2])


def project(edges, weight):
    flat = edges.reshape(-1, edges.shape[-1])
    result = jnp.dot(flat, weight, preferred_element_type=F32).astype(BF)
    return result.reshape(edges.shape[:-1] + (weight.shape[1],))


def compute(
    left_blocks,
    right_blocks,
    cotangent,
    query_weight,
    key_weight,
    left_weight,
    right_weight,
    out_weight,
    left_at,
    right_at,
):
    scaling = 1.0 / math.sqrt(HEAD_DIM)
    rows_local, columns, width = cotangent.shape
    nodes = 256
    hidden_width = HEADS * HEAD_DIM
    lb = left_blocks[left_at]
    rb = right_blocks[right_at]
    gathered_left = lb[:, :128].reshape(16, 8, 16, width).transpose(1, 0, 2, 3).reshape(8, nodes, width)
    gathered_lmask = lb[:, 128:136, :16].transpose(1, 0, 2).reshape(8, nodes)
    gathered_right = rb[:, :256].reshape(16, 16, 16, width).transpose(0, 2, 1, 3).reshape(nodes, 16, width)
    gathered_rmask = rb[:, 256:, :16].transpose(0, 2, 1).reshape(nodes, 16)

    query_heads = project(gathered_left, query_weight).reshape(rows_local, nodes, HEADS, HEAD_DIM)
    left_heads = project(gathered_left, left_weight).reshape(rows_local, nodes, HEADS, HEAD_DIM)
    key_heads = project(gathered_right, key_weight).reshape(nodes, columns, HEADS, HEAD_DIM)
    right_heads = project(gathered_right, right_weight).reshape(nodes, columns, HEADS, HEAD_DIM)
    upstream = jnp.dot(
        cotangent.reshape(-1, width), out_weight.T, preferred_element_type=F32
    ).astype(BF)
    upstream_wide = upstream.reshape(rows_local, columns, HEADS, HEAD_DIM).astype(F32)[
        :, :, None
    ]
    scores = (
        jnp.einsum("ilhe,ljhe->hijl", query_heads, key_heads, preferred_element_type=F32)
        * scaling
    )
    allowed = gathered_lmask[:, None, :] * gathered_rmask.T[None, :, :] > 0
    scores = jnp.where(allowed[None], scores, -1000000000.0)
    highest_score = jnp.max(scores, axis=3, keepdims=True)
    raw_weights = jnp.exp(scores - highest_score)
    weights = raw_weights / jnp.sum(raw_weights, axis=3, keepdims=True)
    weights_low = weights.astype(BF)
    block_size = 64

    def triple_terms(block_index, carry):
        attended_sum, weight_grad, grad_left, grad_right = carry
        offset = block_index * block_size
        left_part = lax.dynamic_slice_in_dim(left_heads, offset, block_size, 1).astype(F32)[
            :, None
        ]
        right_part = jnp.swapaxes(
            lax.dynamic_slice_in_dim(right_heads, offset, block_size, 0), 0, 1
        ).astype(F32)[None]
        weight_part = jnp.transpose(
            lax.dynamic_slice_in_dim(weights_low, offset, block_size, 3), (1, 2, 3, 0)
        ).astype(F32)[..., None]
        value_pair = left_part * right_part
        attended_sum = attended_sum + jnp.sum(weight_part * value_pair, axis=2)
        grad_part = jnp.sum(upstream_wide * value_pair, axis=4)
        weight_grad = lax.dynamic_update_slice_in_dim(
            weight_grad, jnp.transpose(grad_part, (3, 0, 1, 2)), offset, 3
        )
        weighted = weight_part * upstream_wide
        left_piece = jnp.sum(weighted * right_part, axis=1).reshape(
            rows_local, block_size, hidden_width
        )
        right_piece = jnp.swapaxes(jnp.sum(weighted * left_part, axis=0), 0, 1).reshape(
            block_size, columns, hidden_width
        )
        grad_left = lax.dynamic_update_slice_in_dim(grad_left, left_piece, offset, 1)
        grad_right = lax.dynamic_update_slice_in_dim(grad_right, right_piece, offset, 0)
        return (attended_sum, weight_grad, grad_left, grad_right)

    start = (
        jnp.zeros((rows_local, columns, HEADS, HEAD_DIM), F32),
        jnp.zeros(weights.shape, F32),
        jnp.zeros((rows_local, nodes, hidden_width), F32),
        jnp.zeros((nodes, columns, hidden_width), F32),
    )
    attended_sum, weight_grad, grad_left, right_sum = lax.fori_loop(
        0, nodes // block_size, triple_terms, start
    )
    score_grad = (
        weights * (weight_grad - jnp.sum(weights * weight_grad, axis=3, keepdims=True)) * scaling
    )
    score_low = score_grad.astype(BF)
    grad_query = jnp.einsum(
        "hijl,ljhe->ilhe", score_low, key_heads, preferred_element_type=F32
    ).reshape(-1, hidden_width).astype(BF)
    key_sum = jnp.einsum(
        "hijl,ilhe->ljhe", score_low, query_heads, preferred_element_type=F32
    ).reshape(-1, hidden_width).astype(BF)
    grad_left = grad_left.reshape(-1, hidden_width).astype(BF)
    right_sum = right_sum.reshape(-1, hidden_width).astype(BF)
    attended = attended_sum.astype(BF).reshape(-1, hidden_width)

    def both(first, first_weight, second, second_weight):
        return jnp.dot(first, first_weight.T, preferred_element_type=F32) + jnp.dot(
            second, second_weight.T, preferred_element_type=F32
        )

    left_part = both(grad_query, query_weight, grad_left, left_weight).astype(BF)
    right_part = both(key_sum, key_weight, right_sum, right_weight).astype(BF)
    xl = gathered_left.reshape(-1, width)
    xr = gathered_right.reshape(-1, width)
    weight_part = jnp.concatenate(
        [
            jnp.dot(edges.T, grads, preferred_element_type=F32)
            for edges, grads in (
                (xl, grad_query),
                (xr, key_sum),
                (xl, grad_left),
                (xr, right_sum),
                (attended, cotangent.reshape(-1, width)),
            )
        ]
    ).astype(BF)
    left_part = left_part.reshape(8, 16, 16, width).transpose(1, 0, 2, 3).reshape(16, 128, width)
    right_part = right_part.reshape(16, 16, 16, width).transpose(0, 2, 1, 3).reshape(16, 256, width)
    order = jnp.arange(16)
    left_back = jnp.zeros(16, jnp.int32).at[left_at].set(order)
    right_back = jnp.zeros(16, jnp.int32).at[right_at].set(order)
    return left_part[left_back], right_part[right_back], weight_part


def body(
    left_edges,
    right_edges,
    left_mask,
    right_mask,
    cotangent,
    query_weight,
    key_weight,
    left_weight,
    right_weight,
    out_weight,
):
    width = left_edges.shape[2]
    row = lax.axis_index("row")
    col = lax.axis_index("col")
    blocks = jnp.arange(16)
    left_rows = jnp.concatenate(
        [
            left_edges.reshape(-1, width),
            jnp.pad(jnp.tile(left_mask.astype(BF), (1, 8)), ((0, 8), (0, 0))),
        ]
    )
    right_rows = jnp.concatenate(
        [
            jnp.swapaxes(right_edges, 0, 1).reshape(-1, width),
            jnp.tile(right_mask.T.astype(BF), (1, 8)),
        ]
    )
    left_blocks = gather_col(left_rows)
    right_blocks = gather_row(right_rows)
    left_part, right_part, weight_part = compute(
        left_blocks,
        right_blocks,
        cotangent,
        query_weight,
        key_weight,
        left_weight,
        right_weight,
        out_weight,
        left_place(col, blocks),
        right_place(row, blocks),
    )

    chunks = right_part.reshape(4, 1024, width)
    total = add_up(chunks[0], [lax.ppermute(chunks[k], "row", flip(4 * k)) for k in (1, 2, 3)])
    chunks = total.astype(BF).reshape(4, 256, width)
    right_grad = add_up(
        total[:256], [lax.ppermute(chunks[k], "row", flip(k)) for k in (1, 2, 3)]
    )
    right_grad = jnp.swapaxes(right_grad.reshape(16, 16, width), 0, 1)

    core = col & 1
    halves = weight_part.reshape(2, 320, width)
    mine = lax.dynamic_index_in_dim(halves, core, 0, keepdims=False)
    other = lax.dynamic_index_in_dim(halves, 1 - core, 0, keepdims=False)
    sent = jnp.concatenate([left_part[8:].reshape(1024, width), other])
    kept = jnp.concatenate([left_part[:8].reshape(1024, width), mine])
    total = add_up(kept, [lax.ppermute(sent, "col", flip(1))])
    low = total.astype(BF)
    came = [
        lax.ppermute(
            jnp.concatenate([low[256 * k : 256 * k + 256], low[1024:]]), "col", flip(4 * k)
        ).astype(F32)
        for k in (1, 2, 3)
    ]
    kept = jnp.concatenate([total[:256], low[1024:].astype(F32)])
    total = (kept + came[0]) + (came[1] + came[2])
    low = total[128:].astype(BF)
    came = lax.ppermute(low, "col", flip(2)).astype(F32)
    left_grad = total[:128] + came[:128]
    weights = low[128:].astype(F32) + came[128:]
    weights = meet(weights.astype(BF), "row", (4, 8, 12))
    weights = meet(weights.astype(BF), "row", (1, 2, 3))
    mine = weights.astype(BF)
    other = lax.ppermute(mine, "col", flip(1))
    first = jnp.where(core == 0, mine, other)
    second = jnp.where(core == 0, other, mine)
    weights = jnp.concatenate([first, second]).astype(F32)
    proj_grads = weights[:512].reshape(4, 128, width)
    return (left_grad.reshape(left_edges.shape), right_grad, proj_grads, weights[512:])


def solution(mesh):
    return jax.shard_map(
        body,
        mesh=mesh,
        in_specs=(
            P("row", "col", None),
            P("row", "col", None),
            P("row", "col"),
            P("row", "col"),
            P("row", "col", None),
            P(),
            P(),
            P(),
            P(),
            P(),
        ),
        out_specs=(P("row", "col", None), P("row", "col", None), P(), P()),
        check_vma=False,
    )
```

```python
import math

import jax
import jax.numpy as jnp
from jax import lax
from jax.experimental import pallas as pl
from jax.experimental.pallas import tpu as pltpu
from jax.sharding import PartitionSpec as P

HEADS = 4
HEAD_DIM = 32
BF = jnp.bfloat16
F32 = jnp.float32


def flip(k):
    return [(i, i ^ k) for i in range(16)]


def gather_col(block):
    pair = jnp.stack([block, lax.ppermute(block, "col", flip(2))])
    quads = jnp.concatenate([pair] + [lax.ppermute(pair, "col", flip(k)) for k in (4, 8, 12)])
    return quads, lax.ppermute(quads, "col", flip(1))


def gather_row(block):
    line = jnp.stack([block] + [lax.ppermute(block, "row", flip(k)) for k in (1, 2, 3)])
    return [line] + [lax.ppermute(line, "row", flip(k)) for k in (4, 8, 12)]


def left_place(col, b):
    apart = col ^ b
    return (apart & 1) * 8 + (apart >> 2) * 2 + ((apart >> 1) & 1)


def add_up(own, others):
    total = own.astype(F32)
    for other in others:
        total = total + other.astype(F32)
    return total


def meet(own, axis, flips):
    came = [lax.ppermute(own, axis, flip(k)).astype(F32) for k in flips]
    return (own.astype(F32) + came[0]) + (came[1] + came[2])


def nt(a, b):
    return lax.dot_general(a, b, (((1,), (1,)), ((), ())), preferred_element_type=F32)


def nn(a, b):
    return jnp.dot(a, b, preferred_element_type=F32)


def tn(a, b):
    return lax.dot_general(a, b, (((0,), (0,)), ((), ())), preferred_element_type=F32)


def triple_kernel(
    at_ref,
    left0,
    left1,
    right0,
    right1,
    right2,
    right3,
    cot_ref,
    wl_ref,
    wr_ref,
    wo_ref,
    lout,
    rout,
    wout,
    xl,
    xr,
    ql,
    kr,
    gql,
    gkr,
    ub,
    ut,
    ts,
    tg,
    pb,
    sb,
    att,
    wsum,
    rp,
    rmask,
):
    scaling = 1.0 / math.sqrt(HEAD_DIM)
    row = at_ref[0]
    col = at_ref[1]
    lefts = (left0, left1)
    rights = (right0, right1, right2, right3)
    slots = [left_place(col, row ^ t) for t in range(16)]

    lane = lax.broadcasted_iota(jnp.int32, (16, 128), 1) // 16
    half0 = jnp.zeros((16, 128), F32)
    half1 = jnp.zeros((16, 128), F32)
    for t in range(16):
        slot = slots[t]
        block = rights[t // 4]
        for j in range(16):
            xr[j, slot] = block[t % 4, 16 * j : 16 * j + 16, :]
        came = block[t % 4, 256:272, :].astype(F32)
        half0 = jnp.where(lane == slot, came, half0)
        half1 = jnp.where(lane + 8 == slot, came, half1)
    right_allowed = jnp.concatenate([half0, half1], axis=1)
    spread4 = (
        lax.broadcasted_iota(jnp.int32, (64, 16), 0) // 4
        == lax.broadcasted_iota(jnp.int32, (64, 16), 1)
    ).astype(BF)
    rmask[...] = nn(spread4, right_allowed.astype(BF))
    halves = []
    for half in range(2):
        total = jnp.zeros((16, 128), F32)
        for s in range(8):
            total = jnp.where(lane == s, lefts[half][s, 128:144, :].astype(F32), total)
        halves.append(total)
    left_allowed = jnp.concatenate(halves, axis=1)

    wl = wl_ref[...]
    wr = wr_ref[...]
    for i in range(8):
        for s in range(16):
            xl[i, s] = lefts[s // 8][s % 8, 16 * i : 16 * i + 16, :]

    def project_left(i, _):
        ql[i] = nt(wl, xl[i].reshape(256, 128)).astype(BF).astype(F32)
        return 0

    lax.fori_loop(0, 8, project_left, 0)

    def project_right(j, _):
        kr[j] = nt(wr, xr[j].reshape(256, 128)).astype(BF).astype(F32)
        return 0

    lax.fori_loop(0, 16, project_right, 0)
    cot = cot_ref[...]
    ut[...] = nt(wo_ref[...], cot).astype(BF).astype(F32)

    def spread_upstream(t, _):
        rows = pl.ds(pl.multiple_of(t * 8, 8), 8)
        tile = ut[rows, :]
        for ij in range(128):
            ub[ij, rows, :] = jnp.broadcast_to(tile[:, ij : ij + 1], (8, 128))
        return 0

    lax.fori_loop(0, 16, spread_upstream, 0)

    fold8 = (
        lax.broadcasted_iota(jnp.int32, (64, 512), 1) // 8
        == lax.broadcasted_iota(jnp.int32, (64, 512), 0)
    ).astype(BF)
    spread8 = (
        lax.broadcasted_iota(jnp.int32, (512, 64), 0) // 8
        == lax.broadcasted_iota(jnp.int32, (512, 64), 1)
    ).astype(BF)

    for i2 in range(4):
        pair = (2 * i2, 2 * i2 + 1)

        def score_head(h, _, pair=pair):
            tiles = [pl.ds(pl.multiple_of(h * 32 + 8 * e, 8), 8) for e in range(4)]
            lower = [pl.ds(pl.multiple_of(128 + h * 32 + 8 * e, 8), 8) for e in range(4)]
            q = [[ql[i, r, :] for r in tiles] for i in pair]
            v = [[ql[i, r, :] for r in lower] for i in pair]
            for j in range(16):
                k = [kr[j, r, :] for r in tiles]
                w = [kr[j, r, :] for r in lower]
                out = pl.ds(pl.multiple_of((j * 4 + h) * 8, 8), 8)
                for n in range(2):
                    u = [ub[pair[n] * 16 + j, r, :] for r in tiles]
                    u = [jnp.concatenate([x, x], axis=1) for x in u]
                    ts[n, out, :] = (q[n][0] * k[0] + q[n][1] * k[1]) + (
                        q[n][2] * k[2] + q[n][3] * k[3]
                    )
                    tg[n, out, :] = (u[0] * (v[n][0] * w[0]) + u[1] * (v[n][1] * w[1])) + (
                        u[2] * (v[n][2] * w[2]) + u[3] * (v[n][3] * w[3])
                    )
            return 0

        lax.fori_loop(0, 4, score_head, 0)
        for n in range(2):
            i = pair[n]
            part = ts[n]
            high = part.astype(BF)
            low = (part - high.astype(F32)).astype(BF)
            score = (nn(fold8, high) + nn(fold8, low)) * scaling
            grad = nn(fold8, tg[n].astype(BF))
            allowed = rmask[...] * left_allowed[i : i + 1, :] > 0.5
            score = jnp.where(allowed, score, -1000000000.0)
            top = jnp.max(score, axis=1, keepdims=True)
            raw = jnp.exp(score - top)
            prob = raw / jnp.sum(raw, axis=1, keepdims=True)
            mean = jnp.sum(prob * grad, axis=1, keepdims=True)
            grad = prob * (grad - mean) * scaling
            pb[i] = nn(spread8, prob.astype(BF))
            sb[i] = nn(spread8, grad.astype(BF))

    column = lax.broadcasted_iota(jnp.int32, (8, 128), 1)

    def gradients(t, _):
        h = t // 4
        rows = pl.ds(pl.multiple_of(t * 8, 8), 8)
        lower = pl.ds(pl.multiple_of(128 + t * 8, 8), 8)
        seen = jnp.zeros((8, 128), F32)
        for ib in range(2):
            group = range(4 * ib, 4 * ib + 4)
            q = [ql[i, rows, :] for i in group]
            v = [ql[i, lower, :] for i in group]
            gq = [jnp.zeros((8, 256), F32) for _ in group]
            gl = [jnp.zeros((8, 256), F32) for _ in group]
            for j in range(16):
                k = kr[j, rows, :]
                w = kr[j, lower, :]
                at = pl.ds(pl.multiple_of((j * 4 + h) * 8, 8), 8)
                if ib == 0:
                    gk = jnp.zeros((8, 256), F32)
                    gr = jnp.zeros((8, 256), F32)
                else:
                    gk = gkr[j, rows, :]
                    gr = gkr[j, lower, :]
                for n, i in enumerate(group):
                    p = pb[i, at, :]
                    s = sb[i, at, :]
                    u = ub[i * 16 + j, rows, :]
                    pu = p * jnp.concatenate([u, u], axis=1)
                    gl[n] = gl[n] + pu * w
                    gr = gr + pu * v[n]
                    gq[n] = gq[n] + s * k
                    gk = gk + s * q[n]
                    a = p * (v[n] * w)
                    a = jnp.sum(a[:, :128] + a[:, 128:], axis=1, keepdims=True)
                    seen = jnp.where(column == i * 16 + j, a, seen)
                gkr[j, rows, :] = gk
                gkr[j, lower, :] = gr
            for n, i in enumerate(group):
                gql[i, rows, :] = gq[n]
                gql[i, lower, :] = gl[n]
        att[rows, :] = seen
        return 0

    lax.fori_loop(0, 16, gradients, 0)

    wsum[...] = jnp.zeros((512, 128), F32)

    def finish_left(i, _):
        g = gql[i].astype(BF)
        wsum[:256, :] += nn(g, xl[i].reshape(256, 128))
        part = tn(g, wl).astype(BF).reshape(16, 16, 128)
        rows = pl.ds(pl.multiple_of(i * 16, 16), 16)
        for s in range(16):
            lout[s, rows, :] = part[s]
        return 0

    lax.fori_loop(0, 8, finish_left, 0)

    def finish_right(j, _):
        g = gkr[j].astype(BF)
        wsum[256:, :] += nn(g, xr[j].reshape(256, 128))
        rp[...] = tn(g, wr).astype(BF).reshape(16, 16, 128)
        rows = pl.ds(pl.multiple_of(j * 16, 16), 16)
        for t in range(16):
            rout[t, rows, :] = rp[slots[t]]
        return 0

    lax.fori_loop(0, 16, finish_right, 0)
    wout[0:128, :] = wsum[0:128, :].T.astype(BF)
    wout[128:256, :] = wsum[256:384, :].T.astype(BF)
    wout[256:384, :] = wsum[128:256, :].T.astype(BF)
    wout[384:512, :] = wsum[384:512, :].T.astype(BF)
    wout[512:640, :] = nn(att[...].astype(BF), cot).astype(BF)


def triples(at, lefts, rights, cot, wl, wr, wo):
    vmem = pl.BlockSpec(memory_space=pltpu.VMEM)
    return pl.pallas_call(
        triple_kernel,
        out_shape=(
            jax.ShapeDtypeStruct((16, 128, 128), BF),
            jax.ShapeDtypeStruct((16, 256, 128), BF),
            jax.ShapeDtypeStruct((640, 128), BF),
        ),
        in_specs=[pl.BlockSpec(memory_space=pltpu.SMEM)] + [vmem] * 10,
        out_specs=(vmem, vmem, vmem),
        scratch_shapes=[
            pltpu.VMEM((8, 16, 16, 128), BF),
            pltpu.VMEM((16, 16, 16, 128), BF),
            pltpu.VMEM((8, 256, 256), F32),
            pltpu.VMEM((16, 256, 256), F32),
            pltpu.VMEM((8, 256, 256), F32),
            pltpu.VMEM((16, 256, 256), F32),
            pltpu.VMEM((128, 128, 128), F32),
            pltpu.VMEM((128, 128), F32),
            pltpu.VMEM((2, 512, 256), F32),
            pltpu.VMEM((2, 512, 256), F32),
            pltpu.VMEM((8, 512, 256), F32),
            pltpu.VMEM((8, 512, 256), F32),
            pltpu.VMEM((128, 128), F32),
            pltpu.VMEM((512, 128), F32),
            pltpu.VMEM((16, 16, 128), BF),
            pltpu.VMEM((64, 256), F32),
        ],
        compiler_params=pltpu.CompilerParams(vmem_limit_bytes=48 * 1024 * 1024),
        cost_estimate=pl.CostEstimate(
            flops=800_000_000, bytes_accessed=5_000_000, transcendentals=131072
        ),
    )(at, *lefts, *rights, cot, wl, wr, wo)


def body(
    left_edges,
    right_edges,
    left_mask,
    right_mask,
    cotangent,
    query_weight,
    key_weight,
    left_weight,
    right_weight,
    out_weight,
):
    width = left_edges.shape[2]
    row = lax.axis_index("row")
    col = lax.axis_index("col")
    left_rows = jnp.concatenate(
        [
            left_edges.reshape(-1, width),
            jnp.pad(jnp.tile(left_mask.astype(BF), (1, 8)), ((0, 8), (0, 0))),
        ]
    )
    right_rows = jnp.concatenate(
        [
            jnp.swapaxes(right_edges, 0, 1).reshape(-1, width),
            jnp.tile(right_mask.T.astype(BF), (1, 8)),
        ]
    )
    lefts = gather_col(left_rows)
    rights = gather_row(right_rows)
    left_part, right_part, weight_part = triples(
        jnp.stack([row, col]).astype(jnp.int32),
        lefts,
        rights,
        cotangent.reshape(-1, width),
        jnp.concatenate([query_weight.T, left_weight.T]),
        jnp.concatenate([key_weight.T, right_weight.T]),
        out_weight,
    )

    chunks = right_part.reshape(4, 1024, width)
    total = add_up(chunks[0], [lax.ppermute(chunks[k], "row", flip(4 * k)) for k in (1, 2, 3)])
    chunks = total.astype(BF).reshape(4, 256, width)
    right_grad = add_up(
        total[:256], [lax.ppermute(chunks[k], "row", flip(k)) for k in (1, 2, 3)]
    )
    right_grad = jnp.swapaxes(right_grad.reshape(16, 16, width), 0, 1)

    core = col & 1
    halves = weight_part.reshape(2, 320, width)
    mine = lax.dynamic_index_in_dim(halves, core, 0, keepdims=False)
    other = lax.dynamic_index_in_dim(halves, 1 - core, 0, keepdims=False)
    sent = jnp.concatenate([left_part[8:].reshape(1024, width), other])
    kept = jnp.concatenate([left_part[:8].reshape(1024, width), mine])
    total = add_up(kept, [lax.ppermute(sent, "col", flip(1))])
    low = total.astype(BF)
    came = [
        lax.ppermute(
            jnp.concatenate([low[256 * k : 256 * k + 256], low[1024:]]), "col", flip(4 * k)
        ).astype(F32)
        for k in (1, 2, 3)
    ]
    kept = jnp.concatenate([total[:256], low[1024:].astype(F32)])
    total = (kept + came[0]) + (came[1] + came[2])
    low = total[128:].astype(BF)
    came = lax.ppermute(low, "col", flip(2)).astype(F32)
    left_grad = total[:128] + came[:128]
    weights = low[128:].astype(F32) + came[128:]
    weights = meet(weights.astype(BF), "row", (4, 8, 12))
    weights = meet(weights.astype(BF), "row", (1, 2, 3))
    mine = weights.astype(BF)
    other = lax.ppermute(mine, "col", flip(1))
    first = jnp.where(core == 0, mine, other)
    second = jnp.where(core == 0, other, mine)
    weights = jnp.concatenate([first, second]).astype(F32)
    proj_grads = weights[:512].reshape(4, 128, width)
    return (left_grad.reshape(left_edges.shape), right_grad, proj_grads, weights[512:])


def solution(mesh):
    return jax.shard_map(
        body,
        mesh=mesh,
        in_specs=(
            P("row", "col", None),
            P("row", "col", None),
            P("row", "col"),
            P("row", "col"),
            P("row", "col", None),
            P(),
            P(),
            P(),
            P(),
            P(),
        ),
        out_specs=(P("row", "col", None), P("row", "col", None), P(), P()),
        check_vma=False,
    )
```

```python
import math

import jax
import jax.numpy as jnp
from jax import lax
from jax.experimental import pallas as pl
from jax.experimental.pallas import tpu as pltpu
from jax.sharding import PartitionSpec as P

HEADS = 4
HEAD_DIM = 32
BF = jnp.bfloat16
F32 = jnp.float32


def flip(k):
    return [(i, i ^ k) for i in range(16)]


def send(block, axis, k):
    with jax.named_scope("s_" + axis + str(k)):
        return lax.ppermute(block, axis, flip(k))


def gather(left, right):
    line = jnp.stack([right] + [send(right, "row", k) for k in (1, 2, 3)])
    line, left = lax.optimization_barrier((line, left))
    near = send(line, "row", 4)
    far = send(line, "row", 12)
    pair = jnp.stack([left, send(left, "col", 2)])
    near, far, pair = lax.optimization_barrier((near, far, pair))
    first = send(far[:2], "row", 4)
    second = send(near[2:], "row", 12)
    quads = jnp.concatenate([pair] + [send(pair, "col", k) for k in (4, 8, 12)])
    first, second, quads = lax.optimization_barrier((first, second, quads))
    return (quads, send(quads, "col", 1)), (line, near, far, first, second)


def left_place(col, b):
    apart = col ^ b
    return (apart & 1) * 8 + (apart >> 2) * 2 + ((apart >> 1) & 1)


def add_up(own, others):
    total = own.astype(F32)
    for other in others:
        total = total + other.astype(F32)
    return total


def meet(own, axis, flips):
    came = [send(own, axis, k).astype(F32) for k in flips]
    return (own.astype(F32) + came[0]) + (came[1] + came[2])


def nt(a, b):
    return lax.dot_general(a, b, (((1,), (1,)), ((), ())), preferred_element_type=F32)


def nn(a, b):
    return jnp.dot(a, b, preferred_element_type=F32)


def tn(a, b):
    return lax.dot_general(a, b, (((0,), (0,)), ((), ())), preferred_element_type=F32)


def fold(tiles):
    place = lax.broadcasted_iota(jnp.int32, tiles[0].shape, 0)
    low = place < 4
    fours = [
        jnp.where(low, tiles[n], tiles[n + 4])
        + pltpu.roll(jnp.where(low, tiles[n + 4], tiles[n]), 4, 0)
        for n in range(4)
    ]
    low = (place & 2) == 0
    twos = [
        jnp.where(
            low,
            fours[n] + pltpu.roll(fours[n], 6, 0),
            fours[n + 2] + pltpu.roll(fours[n + 2], 2, 0),
        )
        for n in range(2)
    ]
    return jnp.where(
        (place & 1) == 0,
        twos[0] + pltpu.roll(twos[0], 7, 0),
        twos[1] + pltpu.roll(twos[1], 1, 0),
    )


def triple_kernel(
    at_ref,
    left0,
    left1,
    right0,
    right1,
    right3,
    right2a,
    right2b,
    cot_hbm,
    wq_hbm,
    wk_hbm,
    wl_hbm,
    wr_hbm,
    wo_hbm,
    lkeep,
    lsend,
    akeep,
    asend,
    bkeep,
    bsend,
    xl,
    xr,
    ql,
    kr,
    gql,
    gkr,
    ub,
    ts,
    tg,
    pb,
    sb,
    att,
    lb,
    rb,
    rp,
    vr,
    up,
    cot_ref,
    weights,
    arrived,
):
    scaling = 1.0 / math.sqrt(HEAD_DIM)
    copies = [
        pltpu.make_async_copy(ref, weights.at[n], arrived.at[n])
        for n, ref in enumerate((wq_hbm, wl_hbm, wk_hbm, wr_hbm, wo_hbm))
    ]
    copies.append(pltpu.make_async_copy(cot_hbm, cot_ref, arrived.at[5]))
    for copy in copies:
        copy.start()
    row = at_ref[0]
    col = at_ref[1]
    lefts = (left0, left1)
    rights = (
        [(right0, z) for z in range(4)]
        + [(right1, z) for z in range(4)]
        + [(right2a, 0), (right2a, 1), (right2b, 0), (right2b, 1)]
        + [(right3, z) for z in range(4)]
    )
    outs = [None] * 16
    for z in range(2):
        outs[z], outs[12 + z] = (akeep, z), (akeep, 2 + z)
        outs[4 + z], outs[8 + z] = (asend, z), (asend, 2 + z)
        outs[2 + z], outs[6 + z] = (bkeep, z), (bkeep, 2 + z)
        outs[14 + z], outs[10 + z] = (bsend, z), (bsend, 2 + z)
    slots = [left_place(col, row ^ t) for t in range(16)]

    lane = lax.broadcasted_iota(jnp.int32, (16, 128), 1) // 16
    half0 = jnp.zeros((16, 128), F32)
    half1 = jnp.zeros((16, 128), F32)
    for t in range(16):
        slot = slots[t]
        block, z = rights[t]
        for j in range(16):
            xr[j, slot] = block[z, 16 * j : 16 * j + 16, :]
        came = block[z, 256:272, :].astype(F32)
        half0 = jnp.where(lane == slot, came, half0)
        half1 = jnp.where(lane + 8 == slot, came, half1)
    right_allowed = jnp.concatenate([half0, half1], axis=1)
    spread4 = (
        lax.broadcasted_iota(jnp.int32, (64, 16), 0) // 4
        == lax.broadcasted_iota(jnp.int32, (64, 16), 1)
    ).astype(BF)
    right_allowed = nn(spread4, right_allowed.astype(BF))
    halves = []
    for half in range(2):
        total = jnp.zeros((16, 128), F32)
        for s in range(8):
            total = jnp.where(lane == s, lefts[half][s, 128:144, :].astype(F32), total)
        halves.append(total)
    left_allowed = jnp.concatenate(halves, axis=1)

    for i in range(8):
        for s in range(16):
            xl[i, s] = lefts[s // 8][s % 8, 16 * i : 16 * i + 16, :]
    for copy in copies:
        copy.wait()
    wl = jnp.concatenate([weights[0].T, weights[1].T])
    wr = jnp.concatenate([weights[2].T, weights[3].T])

    def project_left(i, _):
        ql[i] = nt(wl, xl[i].reshape(256, 128)).astype(BF).astype(F32)
        return 0

    lax.fori_loop(0, 8, project_left, 0, unroll=4)

    def project_right(j, _):
        kr[j] = nt(wr, xr[j].reshape(256, 128)).astype(BF).astype(F32)
        return 0

    lax.fori_loop(0, 16, project_right, 0, unroll=4)
    cot = cot_ref[...]
    pick = (
        lax.broadcasted_iota(jnp.int32, (16, 2048), 1) // 128
        == lax.broadcasted_iota(jnp.int32, (16, 2048), 0)
    ).astype(BF)
    wo = weights[4]

    up[...] = nt(cot, wo).astype(BF).astype(F32)
    place = lax.broadcasted_iota(jnp.int32, (8, 256), 0)
    heads = lax.broadcasted_iota(jnp.int32, (8, 256), 1) // 32
    agree = place == heads

    def grad_row(i):
        for jj in range(8):
            both = jnp.concatenate(
                [
                    jnp.broadcast_to(up[pl.ds(i * 16 + 2 * jj + n, 1), :], (8, 128))
                    for n in range(2)
                ],
                axis=1,
            )
            both = jnp.where(agree, both, 0.0).astype(BF)
            tg[i, pl.ds(8 * jj, 8), :] = nn(both, vr[i, jj])

    def score_row(i, _):
        mine = cot_ref[pl.ds(pl.multiple_of(i * 16, 16), 16), :]
        spread = nn(nt(wo, mine).astype(BF), pick)
        for j in range(16):
            ub[i * 16 + j] = spread[:, 128 * j : 128 * j + 128]
        grad_row(jnp.maximum(i - 1, 0))
        for h in range(4):
            tiles = [pl.ds(h * 32 + 8 * e, 8) for e in range(4)]
            q = [ql[i, r, :] for r in tiles]
            v = ql[i, pl.ds(128 + h * 32, 32), :]
            for half in range(2):
                scores = []
                for j in range(8 * half, 8 * half + 8):
                    k = [kr[j, r, :] for r in tiles]
                    scores.append((q[0] * k[0] + q[1] * k[1]) + (q[2] * k[2] + q[3] * k[3]))
                    w = kr[j, pl.ds(128 + h * 32, 32), :]
                    vr[i, j // 2, pl.ds(j % 2 * 128 + h * 32, 32), :] = (v * w).astype(BF)
                score = fold(scores)
                for side in range(2):
                    ts[i, side, pl.ds(32 * half + h, 8, stride=4), :] = score[
                        :, 128 * side : 128 * side + 128
                    ]
        return 0

    lax.fori_loop(0, 8, score_row, 0)
    grad_row(7)

    for i in range(8):
        for part in range(2):
            rows = pl.ds(32 * part, 32)
            allowed = right_allowed[32 * part : 32 * part + 32] * left_allowed[i : i + 1, :] > 0.5
            score = jnp.concatenate([ts[i, 0, rows, :], ts[i, 1, rows, :]], axis=1)
            score = jnp.where(allowed, score * scaling, -1000000000.0)
            grad = tg[i, rows, :]
            top = jnp.max(score, axis=1, keepdims=True)
            raw = jnp.exp(score - top)
            prob = raw / jnp.sum(raw, axis=1, keepdims=True)
            mean = jnp.sum(prob * grad, axis=1, keepdims=True)
            grad = prob * (grad - mean) * scaling
            pb[i, rows, :] = prob.astype(BF).astype(F32)
            sb[i, rows, :] = grad.astype(BF).astype(F32)

    agree = agree[:, :128], agree[:, 128:]

    def gradients(t, _):
        h = t // 4
        rows = pl.ds(pl.multiple_of(t * 8, 8), 8)
        lower = pl.ds(pl.multiple_of(128 + t * 8, 8), 8)
        seen = []
        for n in range(8):
            jj = t % 2 * 4 + n // 2
            prob = pb[t // 2, pl.ds(pl.multiple_of(8 * jj, 8), 8), :].astype(BF)
            part = nt(prob, vr[t // 2, jj, pl.ds(n % 2 * 128, 128), :])
            seen.append(jnp.where(agree[n % 2], part, 0.0))
        att[rows, :] = fold(seen)
        for ib in range(2):
            group = range(4 * ib, 4 * ib + 4)
            q = [ql[i, rows, :] for i in group]
            v = [ql[i, lower, :] for i in group]
            gq = [jnp.zeros((8, 256), F32) for _ in group]
            gl = [jnp.zeros((8, 256), F32) for _ in group]
            for j in range(16):
                k = kr[j, rows, :]
                w = kr[j, lower, :]
                at = pl.ds(j * 4 + h, 1)
                if ib == 0:
                    gk = jnp.zeros((8, 256), F32)
                    gr = jnp.zeros((8, 256), F32)
                else:
                    gk = gkr[j, rows, :]
                    gr = gkr[j, lower, :]
                for n, i in enumerate(group):
                    p = jnp.broadcast_to(pb[i, at, :], (8, 256))
                    s = jnp.broadcast_to(sb[i, at, :], (8, 256))
                    u = ub[i * 16 + j, rows, :]
                    pu = p * jnp.concatenate([u, u], axis=1)
                    gl[n] = gl[n] + pu * w
                    gr = gr + pu * v[n]
                    gq[n] = gq[n] + s * k
                    gk = gk + s * q[n]
                gkr[j, rows, :] = gk
                gkr[j, lower, :] = gr
            for n, i in enumerate(group):
                gql[i, rows, :] = gq[n]
                gql[i, lower, :] = gl[n]
        return 0

    lax.fori_loop(0, 16, gradients, 0)

    def finish(n, _):
        g = gql[n].astype(BF)
        lb[:, pl.ds(pl.multiple_of(n * 256, 256), 256)] = g
        part = tn(g, wl).astype(BF).reshape(16, 16, 128)
        for s in range(16):
            rows = pl.ds(pl.multiple_of(s % 8 * 128 + n * 16, 16), 16)
            (lkeep, lsend)[s // 8][rows, :] = part[s]
        for m in range(2):
            j = 2 * n + m
            g = gkr[j].astype(BF)
            rb[:, pl.ds(pl.multiple_of(j * 256, 256), 256)] = g
            rp[j] = tn(g, wr).astype(BF).reshape(16, 16, 128)
            rows = pl.ds(pl.multiple_of(j * 16, 16), 16)
            for t in range(16):
                out, z = outs[t]
                out[z, rows, :] = rp[j, slots[t]]
        return 0

    lax.fori_loop(0, 8, finish, 0, unroll=2)
    lsum = nn(lb[...], xl[...].reshape(2048, 128))
    rsum = nn(rb[...], xr[...].reshape(4096, 128))
    sums = jnp.concatenate(
        [
            lsum[:128].T,
            rsum[:128].T,
            lsum[128:].T,
            rsum[128:].T,
            tn(att[...].astype(BF), cot),
        ]
    )
    even = (col & 1) == 0
    lkeep[1024:1344, :] = jnp.where(even, sums[:320], sums[320:]).astype(BF)
    lsend[1024:1344, :] = jnp.where(even, sums[320:], sums[:320]).astype(BF)


def triples(at, lefts, rights, cot, wq, wk, wl, wr, wo):
    vmem = pl.BlockSpec(memory_space=pltpu.VMEM)
    return pl.pallas_call(
        triple_kernel,
        out_shape=(
            jax.ShapeDtypeStruct((1344, 128), BF),
            jax.ShapeDtypeStruct((1344, 128), BF),
            jax.ShapeDtypeStruct((4, 256, 128), BF),
            jax.ShapeDtypeStruct((4, 256, 128), BF),
            jax.ShapeDtypeStruct((4, 256, 128), BF),
            jax.ShapeDtypeStruct((4, 256, 128), BF),
        ),
        in_specs=[pl.BlockSpec(memory_space=pltpu.SMEM)]
        + [vmem] * 7
        + [pl.BlockSpec(memory_space=pl.ANY)] * 6,
        out_specs=(vmem,) * 6,
        scratch_shapes=[
            pltpu.VMEM((8, 16, 16, 128), BF),
            pltpu.VMEM((16, 16, 16, 128), BF),
            pltpu.VMEM((8, 256, 256), F32),
            pltpu.VMEM((16, 256, 256), F32),
            pltpu.VMEM((8, 256, 256), F32),
            pltpu.VMEM((16, 256, 256), F32),
            pltpu.VMEM((128, 128, 128), F32),
            pltpu.VMEM((8, 2, 64, 128), F32),
            pltpu.VMEM((8, 64, 256), F32),
            pltpu.VMEM((8, 64, 256), F32),
            pltpu.VMEM((8, 64, 256), F32),
            pltpu.VMEM((128, 128), F32),
            pltpu.VMEM((256, 2048), BF),
            pltpu.VMEM((256, 4096), BF),
            pltpu.VMEM((16, 16, 16, 128), BF),
            pltpu.VMEM((8, 8, 256, 256), BF),
            pltpu.VMEM((128, 128), F32),
            pltpu.VMEM((128, 128), BF),
            pltpu.VMEM((5, 128, 128), BF),
            pltpu.SemaphoreType.DMA((6,)),
        ],
        compiler_params=pltpu.CompilerParams(vmem_limit_bytes=48 * 1024 * 1024),
        cost_estimate=pl.CostEstimate(
            flops=800_000_000, bytes_accessed=5_000_000, transcendentals=131072
        ),
    )(at, *lefts, *rights, cot, wq, wk, wl, wr, wo)


def body(
    left_edges,
    right_edges,
    left_mask,
    right_mask,
    cotangent,
    query_weight,
    key_weight,
    left_weight,
    right_weight,
    out_weight,
):
    width = left_edges.shape[2]
    row = lax.axis_index("row")
    col = lax.axis_index("col")
    left_rows = jnp.concatenate(
        [
            left_edges.reshape(-1, width),
            jnp.pad(jnp.tile(left_mask.astype(BF), (1, 8)), ((0, 8), (0, 0))),
        ]
    )
    right_rows = jnp.concatenate(
        [
            jnp.swapaxes(right_edges, 0, 1).reshape(-1, width),
            jnp.tile(right_mask.T.astype(BF), (1, 8)),
        ]
    )
    lefts, rights = gather(left_rows, right_rows)
    left_keep, left_send, first_keep, first_send, second_keep, second_send = triples(
        jnp.stack([row, col]).astype(jnp.int32),
        lefts,
        rights,
        cotangent.reshape(-1, width),
        query_weight,
        key_weight,
        left_weight,
        right_weight,
        out_weight,
    )

    core = col & 1
    first_came = send(first_send, "row", 4)
    second_came = send(second_send, "row", 12)
    left_total = add_up(left_keep, [send(left_send, "col", 1)])
    low = left_total.astype(BF)
    came = [
        send(jnp.concatenate([low[256 * k : 256 * k + 256], low[1024:]]), "col", 4 * k).astype(F32)
        for k in (1, 2, 3)
    ]
    first_came, second_came, came[0] = lax.optimization_barrier((first_came, second_came, came[0]))
    kept = jnp.concatenate([left_total[:256], low[1024:].astype(F32)])
    total = (kept + came[0]) + (came[1] + came[2])
    low = total[128:].astype(BF)
    first = add_up(first_keep, [first_came])
    second = add_up(second_keep, [second_came])
    first_low, second_low, low = lax.optimization_barrier(
        (first[2:].astype(BF), second[2:].astype(BF), low)
    )
    first_came = send(first_low, "row", 12)
    second_came = send(second_low, "row", 4)
    came = send(low, "col", 2).astype(F32)
    left_grad = total[:128] + came[:128]
    weights = low[128:].astype(F32) + came[128:]
    right_total = jnp.concatenate(
        [add_up(first[:2], [first_came]), add_up(second[:2], [second_came])]
    )
    low = right_total.astype(BF)
    weights, low = lax.optimization_barrier((weights.astype(BF), low))
    weights = meet(weights, "row", (4, 8, 12)).astype(BF)
    weights, low = lax.optimization_barrier((weights, low))
    right_came = [send(low[k], "row", k) for k in (2, 1, 3)]
    weights = meet(weights, "row", (1, 2, 3))
    right_grad = right_total[0] + right_came[1].astype(F32) + right_came[0].astype(F32)
    right_grad = right_grad + right_came[2].astype(F32)
    right_grad = jnp.swapaxes(right_grad.reshape(16, 16, width), 0, 1)
    mine = weights.astype(BF)
    other = send(mine, "col", 1)
    first = jnp.where(core == 0, mine, other)
    second = jnp.where(core == 0, other, mine)
    weights = jnp.concatenate([first, second]).astype(F32)
    proj_grads = weights[:512].reshape(4, 128, width)
    return (left_grad.reshape(left_edges.shape), right_grad, proj_grads, weights[512:])


def solution(mesh):
    return jax.shard_map(
        body,
        mesh=mesh,
        in_specs=(
            P("row", "col", None),
            P("row", "col", None),
            P("row", "col"),
            P("row", "col"),
            P("row", "col", None),
            P(),
            P(),
            P(),
            P(),
            P(),
        ),
        out_specs=(P("row", "col", None), P("row", "col", None), P(), P()),
        check_vma=False,
    )
```

```python
import math

import jax
import jax.numpy as jnp
from jax import lax
from jax.experimental import pallas as pl
from jax.experimental.pallas import tpu as pltpu
from jax.sharding import PartitionSpec as P

HEADS = 4
HEAD_DIM = 32
BF = jnp.bfloat16
F32 = jnp.float32


LINES = [[4 * x + z for z in range(4)] for x in range(4)]


def flip(k):
    return [(i, i ^ k) for i in range(16)]


def send(block, axis, k):
    with jax.named_scope("s_" + axis + str(k)):
        return lax.ppermute(block, axis, flip(k))


def gather(left, right):
    line = jnp.stack([right] + [send(right, "row", k) for k in (1, 2, 3)])
    line, left = lax.optimization_barrier((line, left))
    near = send(line, "row", 4)
    far = send(line, "row", 12)
    pair = jnp.stack([left, send(left, "col", 2)])
    near, far, pair = lax.optimization_barrier((near, far, pair))
    first = send(far[:2], "row", 4)
    second = send(near[2:], "row", 12)
    quads = jnp.concatenate([pair] + [send(pair, "col", k) for k in (4, 8, 12)])
    first, second, quads = lax.optimization_barrier((first, second, quads))
    return (quads, send(quads, "col", 1)), (line, near, far, first, second)


def left_place(col, b):
    apart = col ^ b
    return (apart & 1) * 8 + (apart >> 2) * 2 + ((apart >> 1) & 1)


def add_up(own, others):
    total = own.astype(F32)
    for other in others:
        total = total + other.astype(F32)
    return total


def meet(own, axis, flips):
    came = [send(own, axis, k).astype(F32) for k in flips]
    return (own.astype(F32) + came[0]) + (came[1] + came[2])


def nt(a, b):
    return lax.dot_general(a, b, (((1,), (1,)), ((), ())), preferred_element_type=F32)


def nn(a, b):
    return jnp.dot(a, b, preferred_element_type=F32)


def tn(a, b):
    return lax.dot_general(a, b, (((0,), (0,)), ((), ())), preferred_element_type=F32)


def fold(tiles):
    place = lax.broadcasted_iota(jnp.int32, tiles[0].shape, 0)
    low = place < 4
    fours = [
        jnp.where(low, tiles[n], tiles[n + 4])
        + pltpu.roll(jnp.where(low, tiles[n + 4], tiles[n]), 4, 0)
        for n in range(4)
    ]
    low = (place & 2) == 0
    twos = [
        jnp.where(
            low,
            fours[n] + pltpu.roll(fours[n], 6, 0),
            fours[n + 2] + pltpu.roll(fours[n + 2], 2, 0),
        )
        for n in range(2)
    ]
    return jnp.where(
        (place & 1) == 0,
        twos[0] + pltpu.roll(twos[0], 7, 0),
        twos[1] + pltpu.roll(twos[1], 1, 0),
    )


def triple_kernel(
    at_ref,
    left0,
    left1,
    right0,
    right1,
    right3,
    right2a,
    right2b,
    cot_hbm,
    wq_hbm,
    wk_hbm,
    wl_hbm,
    wr_hbm,
    wo_hbm,
    lkeep,
    lsend,
    akeep,
    asend,
    bkeep,
    bsend,
    xl,
    xr,
    ql,
    kr,
    gql,
    gkr,
    ub,
    ts,
    tg,
    pb,
    sb,
    att,
    lb,
    rb,
    rp,
    vr,
    up,
    cot_ref,
    weights,
    arrived,
):
    scaling = 1.0 / math.sqrt(HEAD_DIM)
    copies = [
        pltpu.make_async_copy(ref, weights.at[n], arrived.at[n])
        for n, ref in enumerate((wq_hbm, wl_hbm, wk_hbm, wr_hbm, wo_hbm))
    ]
    copies.append(pltpu.make_async_copy(cot_hbm, cot_ref, arrived.at[5]))
    for copy in copies:
        copy.start()
    row = at_ref[0]
    col = at_ref[1]
    lefts = (left0, left1)
    rights = (
        [(right0, z) for z in range(4)]
        + [(right1, z) for z in range(4)]
        + [(right2a, 0), (right2a, 1), (right2b, 0), (right2b, 1)]
        + [(right3, z) for z in range(4)]
    )
    outs = [None] * 16
    for z in range(2):
        outs[z], outs[12 + z] = (akeep, z), (akeep, 2 + z)
        outs[4 + z], outs[8 + z] = (asend, z), (asend, 2 + z)
        outs[2 + z], outs[6 + z] = (bkeep, z), (bkeep, 2 + z)
        outs[14 + z], outs[10 + z] = (bsend, z), (bsend, 2 + z)
    slots = [left_place(col, row ^ t) for t in range(16)]

    lane = lax.broadcasted_iota(jnp.int32, (16, 128), 1) // 16
    half0 = jnp.zeros((16, 128), F32)
    half1 = jnp.zeros((16, 128), F32)
    for t in range(16):
        slot = slots[t]
        block, z = rights[t]
        for j in range(16):
            xr[j, slot] = block[z, 16 * j : 16 * j + 16, :]
        came = block[z, 256:272, :].astype(F32)
        half0 = jnp.where(lane == slot, came, half0)
        half1 = jnp.where(lane + 8 == slot, came, half1)
    right_allowed = jnp.concatenate([half0, half1], axis=1)
    spread4 = (
        lax.broadcasted_iota(jnp.int32, (64, 16), 0) // 4
        == lax.broadcasted_iota(jnp.int32, (64, 16), 1)
    ).astype(BF)
    right_allowed = nn(spread4, right_allowed.astype(BF))
    halves = []
    for half in range(2):
        total = jnp.zeros((16, 128), F32)
        for s in range(8):
            total = jnp.where(lane == s, lefts[half][s, 128:144, :].astype(F32), total)
        halves.append(total)
    left_allowed = jnp.concatenate(halves, axis=1)

    for i in range(8):
        for s in range(16):
            xl[i, s] = lefts[s // 8][s % 8, 16 * i : 16 * i + 16, :]
    for copy in copies:
        copy.wait()
    wl = jnp.concatenate([weights[0].T, weights[1].T])
    wr = jnp.concatenate([weights[2].T, weights[3].T])

    def project_left(i, _):
        ql[i] = nt(wl, xl[i].reshape(256, 128)).astype(BF).astype(F32)
        return 0

    lax.fori_loop(0, 8, project_left, 0, unroll=8)

    def project_right(j, _):
        kr[j] = nt(wr, xr[j].reshape(256, 128)).astype(BF).astype(F32)
        return 0

    lax.fori_loop(0, 16, project_right, 0, unroll=8)
    cot = cot_ref[...]
    pick = (
        lax.broadcasted_iota(jnp.int32, (16, 2048), 1) // 128
        == lax.broadcasted_iota(jnp.int32, (16, 2048), 0)
    ).astype(BF)
    wo = weights[4]

    up[...] = nt(cot, wo).astype(BF).astype(F32)
    place = lax.broadcasted_iota(jnp.int32, (8, 256), 0)
    heads = lax.broadcasted_iota(jnp.int32, (8, 256), 1) // 32
    agree = place == heads

    def grad_row(i):
        for jj in range(8):
            both = jnp.concatenate(
                [
                    jnp.broadcast_to(up[pl.ds(i * 16 + 2 * jj + n, 1), :], (8, 128))
                    for n in range(2)
                ],
                axis=1,
            )
            both = jnp.where(agree, both, 0.0).astype(BF)
            tg[i, pl.ds(8 * jj, 8), :] = nn(both, vr[i, jj])

    def score_row(i, _):
        mine = cot_ref[pl.ds(pl.multiple_of(i * 16, 16), 16), :]
        spread = nn(nt(wo, mine).astype(BF), pick)
        for j in range(16):
            ub[i * 16 + j] = spread[:, 128 * j : 128 * j + 128]
        grad_row(jnp.maximum(i - 1, 0))
        for h in range(4):
            tiles = [pl.ds(h * 32 + 8 * e, 8) for e in range(4)]
            q = [ql[i, r, :] for r in tiles]
            v = ql[i, pl.ds(128 + h * 32, 32), :]
            for half in range(2):
                scores = []
                for j in range(8 * half, 8 * half + 8):
                    k = [kr[j, r, :] for r in tiles]
                    scores.append((q[0] * k[0] + q[1] * k[1]) + (q[2] * k[2] + q[3] * k[3]))
                    w = kr[j, pl.ds(128 + h * 32, 32), :]
                    vr[i, j // 2, pl.ds(j % 2 * 128 + h * 32, 32), :] = (v * w).astype(BF)
                score = fold(scores)
                for side in range(2):
                    ts[i, side, pl.ds(32 * half + h, 8, stride=4), :] = score[
                        :, 128 * side : 128 * side + 128
                    ]
        return 0

    lax.fori_loop(0, 8, score_row, 0)
    grad_row(7)

    for i in range(8):
        for part in range(2):
            rows = pl.ds(32 * part, 32)
            allowed = right_allowed[32 * part : 32 * part + 32] * left_allowed[i : i + 1, :] > 0.5
            score = jnp.concatenate([ts[i, 0, rows, :], ts[i, 1, rows, :]], axis=1)
            score = jnp.where(allowed, score * scaling, -1000000000.0)
            grad = tg[i, rows, :]
            top = jnp.max(score, axis=1, keepdims=True)
            raw = jnp.exp(score - top)
            prob = raw / jnp.sum(raw, axis=1, keepdims=True)
            mean = jnp.sum(prob * grad, axis=1, keepdims=True)
            grad = prob * (grad - mean) * scaling
            pb[i, rows, :] = prob.astype(BF).astype(F32)
            sb[i, rows, :] = grad.astype(BF).astype(F32)

    def gradients(t, _):
        h = t // 4
        rows = pl.ds(pl.multiple_of(t * 8, 8), 8)
        lower = pl.ds(pl.multiple_of(128 + t * 8, 8), 8)
        seen = []
        for n in range(4):
            jj = t % 2 * 4 + n
            prob = pb[t // 2, pl.ds(pl.multiple_of(8 * jj, 8), 8), :].astype(BF)
            part = jnp.where(agree, nt(prob, vr[t // 2, jj]), 0.0)
            seen += [part[:, :128], part[:, 128:]]
        att[rows, :] = fold(seen)
        for ib in range(2):
            group = range(4 * ib, 4 * ib + 4)
            q = [ql[i, rows, :] for i in group]
            v = [ql[i, lower, :] for i in group]
            gq = [jnp.zeros((8, 256), F32) for _ in group]
            gl = [jnp.zeros((8, 256), F32) for _ in group]
            for j in range(16):
                k = kr[j, rows, :]
                w = kr[j, lower, :]
                at = pl.ds(j * 4 + h, 1)
                if ib == 0:
                    gk = jnp.zeros((8, 256), F32)
                    gr = jnp.zeros((8, 256), F32)
                else:
                    gk = gkr[j, rows, :]
                    gr = gkr[j, lower, :]
                for n, i in enumerate(group):
                    p = jnp.broadcast_to(pb[i, at, :], (8, 256))
                    s = jnp.broadcast_to(sb[i, at, :], (8, 256))
                    u = ub[i * 16 + j, rows, :]
                    pu = p * jnp.concatenate([u, u], axis=1)
                    gl[n] = gl[n] + pu * w
                    gr = gr + pu * v[n]
                    gq[n] = gq[n] + s * k
                    gk = gk + s * q[n]
                gkr[j, rows, :] = gk
                gkr[j, lower, :] = gr
            for n, i in enumerate(group):
                gql[i, rows, :] = gq[n]
                gql[i, lower, :] = gl[n]
        return 0

    lax.fori_loop(0, 16, gradients, 0)

    def finish(n, _):
        g = gql[n].astype(BF)
        lb[:, pl.ds(pl.multiple_of(n * 256, 256), 256)] = g
        part = tn(g, wl).astype(BF).reshape(16, 16, 128)
        for s in range(16):
            rows = pl.ds(pl.multiple_of(s % 8 * 128 + n * 16, 16), 16)
            (lkeep, lsend)[s // 8][rows, :] = part[s]
        for m in range(2):
            j = 2 * n + m
            g = gkr[j].astype(BF)
            rb[:, pl.ds(pl.multiple_of(j * 256, 256), 256)] = g
            rp[j] = tn(g, wr).astype(BF).reshape(16, 16, 128)
            rows = pl.ds(pl.multiple_of(j * 16, 16), 16)
            for t in range(16):
                out, z = outs[t]
                out[z, rows, :] = rp[j, left_place(col, row // 4 * 4 ^ t)]
        return 0

    lax.fori_loop(0, 8, finish, 0, unroll=4)
    lsum = nn(lb[...], xl[...].reshape(2048, 128))
    rsum = nn(rb[...], xr[...].reshape(4096, 128))
    sums = jnp.concatenate(
        [
            lsum[:128].T,
            rsum[:128].T,
            lsum[128:].T,
            rsum[128:].T,
            tn(att[...].astype(BF), cot),
        ]
    )
    even = (col & 1) == 0
    lkeep[1024:1344, :] = jnp.where(even, sums[:320], sums[320:]).astype(BF)
    lsend[1024:1344, :] = jnp.where(even, sums[320:], sums[:320]).astype(BF)


def triples(at, lefts, rights, cot, wq, wk, wl, wr, wo):
    vmem = pl.BlockSpec(memory_space=pltpu.VMEM)
    return pl.pallas_call(
        triple_kernel,
        out_shape=(
            jax.ShapeDtypeStruct((1344, 128), BF),
            jax.ShapeDtypeStruct((1344, 128), BF),
            jax.ShapeDtypeStruct((4, 256, 128), BF),
            jax.ShapeDtypeStruct((4, 256, 128), BF),
            jax.ShapeDtypeStruct((4, 256, 128), BF),
            jax.ShapeDtypeStruct((4, 256, 128), BF),
        ),
        in_specs=[pl.BlockSpec(memory_space=pltpu.SMEM)]
        + [vmem] * 7
        + [pl.BlockSpec(memory_space=pl.ANY)] * 6,
        out_specs=(vmem,) * 6,
        scratch_shapes=[
            pltpu.VMEM((8, 16, 16, 128), BF),
            pltpu.VMEM((16, 16, 16, 128), BF),
            pltpu.VMEM((8, 256, 256), F32),
            pltpu.VMEM((16, 256, 256), F32),
            pltpu.VMEM((8, 256, 256), F32),
            pltpu.VMEM((16, 256, 256), F32),
            pltpu.VMEM((128, 128, 128), F32),
            pltpu.VMEM((8, 2, 64, 128), F32),
            pltpu.VMEM((8, 64, 256), F32),
            pltpu.VMEM((8, 64, 256), F32),
            pltpu.VMEM((8, 64, 256), F32),
            pltpu.VMEM((128, 128), F32),
            pltpu.VMEM((256, 2048), BF),
            pltpu.VMEM((256, 4096), BF),
            pltpu.VMEM((16, 16, 16, 128), BF),
            pltpu.VMEM((8, 8, 256, 256), BF),
            pltpu.VMEM((128, 128), F32),
            pltpu.VMEM((128, 128), BF),
            pltpu.VMEM((5, 128, 128), BF),
            pltpu.SemaphoreType.DMA((6,)),
        ],
        compiler_params=pltpu.CompilerParams(vmem_limit_bytes=48 * 1024 * 1024),
        cost_estimate=pl.CostEstimate(
            flops=800_000_000, bytes_accessed=5_000_000, transcendentals=131072
        ),
    )(at, *lefts, *rights, cot, wq, wk, wl, wr, wo)


def body(
    left_edges,
    right_edges,
    left_mask,
    right_mask,
    cotangent,
    query_weight,
    key_weight,
    left_weight,
    right_weight,
    out_weight,
):
    width = left_edges.shape[2]
    row = lax.axis_index("row")
    col = lax.axis_index("col")
    left_rows = jnp.concatenate(
        [
            left_edges.reshape(-1, width),
            jnp.pad(jnp.tile(left_mask.astype(BF), (1, 8)), ((0, 8), (0, 0))),
        ]
    )
    right_rows = jnp.concatenate(
        [
            jnp.swapaxes(right_edges, 0, 1).reshape(-1, width),
            jnp.tile(right_mask.T.astype(BF), (1, 8)),
        ]
    )
    lefts, rights = gather(left_rows, right_rows)
    left_keep, left_send, first_keep, first_send, second_keep, second_send = triples(
        jnp.stack([row, col]).astype(jnp.int32),
        lefts,
        rights,
        cotangent.reshape(-1, width),
        query_weight,
        key_weight,
        left_weight,
        right_weight,
        out_weight,
    )

    core = col & 1
    first_came = send(first_send, "row", 4)
    second_came = send(second_send, "row", 12)
    left_total = add_up(left_keep, [send(left_send, "col", 1)])
    low = left_total.astype(BF)
    came = [
        send(jnp.concatenate([low[256 * k : 256 * k + 256], low[1024:]]), "col", 4 * k).astype(F32)
        for k in (1, 2, 3)
    ]
    first_came, second_came, came[0] = lax.optimization_barrier((first_came, second_came, came[0]))
    kept = jnp.concatenate([left_total[:256], low[1024:].astype(F32)])
    total = (kept + came[0]) + (came[1] + came[2])
    low = total[128:].astype(BF)
    first = add_up(first_keep, [first_came])
    second = add_up(second_keep, [second_came])
    first_came = send(first[2:].astype(BF), "row", 12)
    second_came = send(second[2:].astype(BF), "row", 4)
    first_came, second_came, low = lax.optimization_barrier((first_came, second_came, low))
    came = send(low, "col", 2).astype(F32)
    left_grad = total[:128] + came[:128]
    weights = low[128:].astype(F32) + came[128:]
    right_total = jnp.concatenate(
        [add_up(first[:2], [first_came]), add_up(second[:2], [second_came])]
    )
    low = right_total.astype(BF)
    right_came = lax.all_to_all(low, "row", 0, 0, axis_index_groups=LINES)
    weights = meet(weights.astype(BF), "row", (4, 8, 12)).astype(BF)
    right_came, weights = lax.optimization_barrier((right_came, weights))
    weights = meet(weights, "row", (1, 2, 3))
    right_grad = jnp.sum(right_came.astype(F32), axis=0)
    right_grad = jnp.swapaxes(right_grad.reshape(16, 16, width), 0, 1)
    mine = weights.astype(BF)
    other = send(mine, "col", 1)
    first = jnp.where(core == 0, mine, other)
    second = jnp.where(core == 0, other, mine)
    weights = jnp.concatenate([first, second]).astype(F32)
    proj_grads = weights[:512].reshape(4, 128, width)
    return (left_grad.reshape(left_edges.shape), right_grad, proj_grads, weights[512:])


def solution(mesh):
    return jax.shard_map(
        body,
        mesh=mesh,
        in_specs=(
            P("row", "col", None),
            P("row", "col", None),
            P("row", "col"),
            P("row", "col"),
            P("row", "col", None),
            P(),
            P(),
            P(),
            P(),
            P(),
        ),
        out_specs=(P("row", "col", None), P("row", "col", None), P(), P()),
        check_vma=False,
    )
```

```python
import math

import jax
import jax.numpy as jnp
from jax import lax
from jax.experimental import pallas as pl
from jax.experimental.pallas import tpu as pltpu
from jax.sharding import PartitionSpec as P

HEADS = 4
HEAD_DIM = 32
BF = jnp.bfloat16
F32 = jnp.float32


LINES = [[4 * x + z for z in range(4)] for x in range(4)]


def flip(k):
    return [(i, i ^ k) for i in range(16)]


def send(block, axis, k):
    with jax.named_scope("s_" + axis + str(k)):
        return lax.ppermute(block, axis, flip(k))


def gather(left, right):
    line = jnp.stack([right] + [send(right, "row", k) for k in (1, 2, 3)])
    line, left = lax.optimization_barrier((line, left))
    near = send(line, "row", 4)
    far = send(line, "row", 12)
    pair = jnp.stack([left, send(left, "col", 2)])
    near, far, pair = lax.optimization_barrier((near, far, pair))
    first = send(far[:2], "row", 4)
    second = send(near[2:], "row", 12)
    quads = jnp.concatenate([pair] + [send(pair, "col", k) for k in (4, 8, 12)])
    first, second, quads = lax.optimization_barrier((first, second, quads))
    return (quads, send(quads, "col", 1)), (line, near, far, first, second)


def left_place(col, b):
    apart = col ^ b
    return (apart & 1) * 8 + (apart >> 2) * 2 + ((apart >> 1) & 1)


def add_up(own, others):
    total = own.astype(F32)
    for other in others:
        total = total + other.astype(F32)
    return total


def meet(own, axis, flips):
    came = [send(own, axis, k).astype(F32) for k in flips]
    return (own.astype(F32) + came[0]) + (came[1] + came[2])


def nt(a, b):
    return lax.dot_general(a, b, (((1,), (1,)), ((), ())), preferred_element_type=F32)


def nn(a, b):
    return jnp.dot(a, b, preferred_element_type=F32)


def tn(a, b):
    return lax.dot_general(a, b, (((0,), (0,)), ((), ())), preferred_element_type=F32)


def fold(tiles):
    place = lax.broadcasted_iota(jnp.int32, tiles[0].shape, 0)
    low = place < 4
    fours = [
        jnp.where(low, tiles[n], tiles[n + 4])
        + pltpu.roll(jnp.where(low, tiles[n + 4], tiles[n]), 4, 0)
        for n in range(4)
    ]
    low = (place & 2) == 0
    twos = [
        jnp.where(
            low,
            fours[n] + pltpu.roll(fours[n], 6, 0),
            fours[n + 2] + pltpu.roll(fours[n + 2], 2, 0),
        )
        for n in range(2)
    ]
    return jnp.where(
        (place & 1) == 0,
        twos[0] + pltpu.roll(twos[0], 7, 0),
        twos[1] + pltpu.roll(twos[1], 1, 0),
    )


def triple_kernel(
    at_ref,
    left0,
    left1,
    right0,
    right1,
    right3,
    right2a,
    right2b,
    cot_hbm,
    wq_hbm,
    wk_hbm,
    wl_hbm,
    wr_hbm,
    wo_hbm,
    lkeep,
    lsend,
    akeep,
    asend,
    bkeep,
    bsend,
    xl,
    xr,
    ql,
    kr,
    gql,
    gkr,
    ub,
    ts,
    tg,
    pb,
    sb,
    att,
    lb,
    rb,
    rp,
    vr,
    up,
    vb,
    wb,
    cot_ref,
    weights,
    arrived,
):
    scaling = 1.0 / math.sqrt(HEAD_DIM)
    copies = [
        pltpu.make_async_copy(ref, weights.at[n], arrived.at[n])
        for n, ref in enumerate((wq_hbm, wl_hbm, wk_hbm, wr_hbm, wo_hbm))
    ]
    copies.append(pltpu.make_async_copy(cot_hbm, cot_ref, arrived.at[5]))
    for copy in copies:
        copy.start()
    row = at_ref[0]
    col = at_ref[1]
    lefts = (left0, left1)
    rights = (
        [(right0, z) for z in range(4)]
        + [(right1, z) for z in range(4)]
        + [(right2a, 0), (right2a, 1), (right2b, 0), (right2b, 1)]
        + [(right3, z) for z in range(4)]
    )
    outs = [None] * 16
    for z in range(2):
        outs[z], outs[12 + z] = (akeep, z), (akeep, 2 + z)
        outs[4 + z], outs[8 + z] = (asend, z), (asend, 2 + z)
        outs[2 + z], outs[6 + z] = (bkeep, z), (bkeep, 2 + z)
        outs[14 + z], outs[10 + z] = (bsend, z), (bsend, 2 + z)
    slots = [left_place(col, row ^ t) for t in range(16)]

    lane = lax.broadcasted_iota(jnp.int32, (16, 128), 1) // 16
    half0 = jnp.zeros((16, 128), F32)
    half1 = jnp.zeros((16, 128), F32)
    for t in range(16):
        slot = slots[t]
        block, z = rights[t]
        for j in range(16):
            xr[j, slot] = block[z, 16 * j : 16 * j + 16, :]
        came = block[z, 256:272, :].astype(F32)
        half0 = jnp.where(lane == slot, came, half0)
        half1 = jnp.where(lane + 8 == slot, came, half1)
    right_allowed = jnp.concatenate([half0, half1], axis=1)
    spread4 = (
        lax.broadcasted_iota(jnp.int32, (64, 16), 0) // 4
        == lax.broadcasted_iota(jnp.int32, (64, 16), 1)
    ).astype(BF)
    right_allowed = nn(spread4, right_allowed.astype(BF))
    halves = []
    for half in range(2):
        total = jnp.zeros((16, 128), F32)
        for s in range(8):
            total = jnp.where(lane == s, lefts[half][s, 128:144, :].astype(F32), total)
        halves.append(total)
    left_allowed = jnp.concatenate(halves, axis=1)

    for i in range(8):
        for s in range(16):
            xl[i, s] = lefts[s // 8][s % 8, 16 * i : 16 * i + 16, :]
    for copy in copies:
        copy.wait()
    wl = jnp.concatenate([weights[0].T, weights[1].T])
    wr = jnp.concatenate([weights[2].T, weights[3].T])

    def project_left(i, _):
        both = nt(wl, xl[i].reshape(256, 128)).astype(BF)
        ql[i] = both.astype(F32)
        vb[i] = both[128:]
        return 0

    lax.fori_loop(0, 8, project_left, 0, unroll=8)

    def project_right(j, _):
        both = nt(wr, xr[j].reshape(256, 128)).astype(BF)
        kr[j] = both.astype(F32)
        wb[j] = both[128:]
        return 0

    lax.fori_loop(0, 16, project_right, 0, unroll=8)
    cot = cot_ref[...]
    pick = (
        lax.broadcasted_iota(jnp.int32, (16, 2048), 1) // 128
        == lax.broadcasted_iota(jnp.int32, (16, 2048), 0)
    ).astype(BF)
    wo = weights[4]

    up[...] = nt(cot, wo).astype(BF).astype(F32)
    place = lax.broadcasted_iota(jnp.int32, (8, 256), 0)
    heads = lax.broadcasted_iota(jnp.int32, (8, 256), 1) // 32
    agree = place == heads

    def grad_row(i):
        for jj in range(8):
            both = jnp.concatenate(
                [
                    jnp.broadcast_to(up[pl.ds(i * 16 + 2 * jj + n, 1), :], (8, 128))
                    for n in range(2)
                ],
                axis=1,
            )
            both = jnp.where(agree, both, 0.0).astype(BF)
            tg[i, pl.ds(8 * jj, 8), :] = nn(both, vr[i, jj])

    def score_row(i, _):
        mine = cot_ref[pl.ds(pl.multiple_of(i * 16, 16), 16), :]
        spread = nn(nt(wo, mine).astype(BF), pick)
        for j in range(16):
            ub[i * 16 + j] = spread[:, 128 * j : 128 * j + 128]
        grad_row(jnp.maximum(i - 1, 0))
        for h in range(4):
            tiles = [pl.ds(h * 32 + 8 * e, 8) for e in range(4)]
            q = [ql[i, r, :] for r in tiles]
            v = vb[i, pl.ds(h * 32, 32), :]
            for half in range(2):
                scores = []
                for j in range(8 * half, 8 * half + 8):
                    k = [kr[j, r, :] for r in tiles]
                    scores.append((q[0] * k[0] + q[1] * k[1]) + (q[2] * k[2] + q[3] * k[3]))
                    w = wb[j, pl.ds(h * 32, 32), :]
                    vr[i, j // 2, pl.ds(j % 2 * 128 + h * 32, 32), :] = v * w
                score = fold(scores)
                for side in range(2):
                    ts[i, side, pl.ds(32 * half + h, 8, stride=4), :] = score[
                        :, 128 * side : 128 * side + 128
                    ]
        return 0

    lax.fori_loop(0, 8, score_row, 0, unroll=2)
    grad_row(7)

    for i in range(8):
        for part in range(2):
            rows = pl.ds(32 * part, 32)
            allowed = right_allowed[32 * part : 32 * part + 32] * left_allowed[i : i + 1, :] > 0.5
            score = jnp.concatenate([ts[i, 0, rows, :], ts[i, 1, rows, :]], axis=1)
            score = jnp.where(allowed, score * scaling, -1000000000.0)
            grad = tg[i, rows, :]
            top = jnp.max(score, axis=1, keepdims=True)
            raw = jnp.exp(score - top)
            prob = raw / jnp.sum(raw, axis=1, keepdims=True)
            mean = jnp.sum(prob * grad, axis=1, keepdims=True)
            grad = prob * (grad - mean) * scaling
            pb[i, rows, :] = prob.astype(BF).astype(F32)
            sb[i, rows, :] = grad.astype(BF).astype(F32)

    def gradients(t, _):
        h = t // 4
        rows = pl.ds(pl.multiple_of(t * 8, 8), 8)
        lower = pl.ds(pl.multiple_of(128 + t * 8, 8), 8)
        seen = []
        for n in range(4):
            jj = t % 2 * 4 + n
            prob = pb[t // 2, pl.ds(pl.multiple_of(8 * jj, 8), 8), :].astype(BF)
            part = jnp.where(agree, nt(prob, vr[t // 2, jj]), 0.0)
            seen += [part[:, :128], part[:, 128:]]
        att[rows, :] = fold(seen)
        for ib in range(2):
            group = range(4 * ib, 4 * ib + 4)
            q = [ql[i, rows, :] for i in group]
            v = [ql[i, lower, :] for i in group]
            gq = [jnp.zeros((8, 256), F32) for _ in group]
            gl = [jnp.zeros((8, 256), F32) for _ in group]
            for j in range(16):
                k = kr[j, rows, :]
                w = kr[j, lower, :]
                at = pl.ds(j * 4 + h, 1)
                if ib == 0:
                    gk = jnp.zeros((8, 256), F32)
                    gr = jnp.zeros((8, 256), F32)
                else:
                    gk = gkr[j, rows, :]
                    gr = gkr[j, lower, :]
                for n, i in enumerate(group):
                    p = jnp.broadcast_to(pb[i, at, :], (8, 256))
                    s = jnp.broadcast_to(sb[i, at, :], (8, 256))
                    u = ub[i * 16 + j, rows, :]
                    pu = p * jnp.concatenate([u, u], axis=1)
                    gl[n] = gl[n] + pu * w
                    gr = gr + pu * v[n]
                    gq[n] = gq[n] + s * k
                    gk = gk + s * q[n]
                gkr[j, rows, :] = gk
                gkr[j, lower, :] = gr
            for n, i in enumerate(group):
                gql[i, rows, :] = gq[n]
                gql[i, lower, :] = gl[n]
        return 0

    lax.fori_loop(0, 16, gradients, 0)

    def finish(n, _):
        g = gql[n].astype(BF)
        lb[:, pl.ds(pl.multiple_of(n * 256, 256), 256)] = g
        part = tn(g, wl).astype(BF).reshape(16, 16, 128)
        for s in range(16):
            rows = pl.ds(pl.multiple_of(s % 8 * 128 + n * 16, 16), 16)
            (lkeep, lsend)[s // 8][rows, :] = part[s]
        for m in range(2):
            j = 2 * n + m
            g = gkr[j].astype(BF)
            rb[:, pl.ds(pl.multiple_of(j * 256, 256), 256)] = g
            rp[j] = tn(g, wr).astype(BF).reshape(16, 16, 128)
            rows = pl.ds(pl.multiple_of(j * 16, 16), 16)
            for t in range(16):
                out, z = outs[t]
                out[z, rows, :] = rp[j, left_place(col, row // 4 * 4 ^ t)]
        return 0

    lax.fori_loop(0, 8, finish, 0, unroll=8)
    lsum = nn(lb[...], xl[...].reshape(2048, 128))
    rsum = nn(rb[...], xr[...].reshape(4096, 128))
    sums = jnp.concatenate(
        [
            lsum[:128].T,
            rsum[:128].T,
            lsum[128:].T,
            rsum[128:].T,
            tn(att[...].astype(BF), cot),
        ]
    )
    even = (col & 1) == 0
    lkeep[1024:1344, :] = jnp.where(even, sums[:320], sums[320:]).astype(BF)
    lsend[1024:1344, :] = jnp.where(even, sums[320:], sums[:320]).astype(BF)


def triples(at, lefts, rights, cot, wq, wk, wl, wr, wo):
    vmem = pl.BlockSpec(memory_space=pltpu.VMEM)
    return pl.pallas_call(
        triple_kernel,
        out_shape=(
            jax.ShapeDtypeStruct((1344, 128), BF),
            jax.ShapeDtypeStruct((1344, 128), BF),
            jax.ShapeDtypeStruct((4, 256, 128), BF),
            jax.ShapeDtypeStruct((4, 256, 128), BF),
            jax.ShapeDtypeStruct((4, 256, 128), BF),
            jax.ShapeDtypeStruct((4, 256, 128), BF),
        ),
        in_specs=[pl.BlockSpec(memory_space=pltpu.SMEM)]
        + [vmem] * 7
        + [pl.BlockSpec(memory_space=pl.ANY)] * 6,
        out_specs=(vmem,) * 6,
        scratch_shapes=[
            pltpu.VMEM((8, 16, 16, 128), BF),
            pltpu.VMEM((16, 16, 16, 128), BF),
            pltpu.VMEM((8, 256, 256), F32),
            pltpu.VMEM((16, 256, 256), F32),
            pltpu.VMEM((8, 256, 256), F32),
            pltpu.VMEM((16, 256, 256), F32),
            pltpu.VMEM((128, 128, 128), F32),
            pltpu.VMEM((8, 2, 64, 128), F32),
            pltpu.VMEM((8, 64, 256), F32),
            pltpu.VMEM((8, 64, 256), F32),
            pltpu.VMEM((8, 64, 256), F32),
            pltpu.VMEM((128, 128), F32),
            pltpu.VMEM((256, 2048), BF),
            pltpu.VMEM((256, 4096), BF),
            pltpu.VMEM((16, 16, 16, 128), BF),
            pltpu.VMEM((8, 8, 256, 256), BF),
            pltpu.VMEM((128, 128), F32),
            pltpu.VMEM((8, 128, 256), BF),
            pltpu.VMEM((16, 128, 256), BF),
            pltpu.VMEM((128, 128), BF),
            pltpu.VMEM((5, 128, 128), BF),
            pltpu.SemaphoreType.DMA((6,)),
        ],
        compiler_params=pltpu.CompilerParams(vmem_limit_bytes=48 * 1024 * 1024),
        cost_estimate=pl.CostEstimate(
            flops=800_000_000, bytes_accessed=5_000_000, transcendentals=131072
        ),
    )(at, *lefts, *rights, cot, wq, wk, wl, wr, wo)


def body(
    left_edges,
    right_edges,
    left_mask,
    right_mask,
    cotangent,
    query_weight,
    key_weight,
    left_weight,
    right_weight,
    out_weight,
):
    width = left_edges.shape[2]
    row = lax.axis_index("row")
    col = lax.axis_index("col")
    left_rows = jnp.concatenate(
        [
            left_edges.reshape(-1, width),
            jnp.pad(jnp.tile(left_mask.astype(BF), (1, 8)), ((0, 8), (0, 0))),
        ]
    )
    right_rows = jnp.concatenate(
        [
            jnp.swapaxes(right_edges, 0, 1).reshape(-1, width),
            jnp.tile(right_mask.T.astype(BF), (1, 8)),
        ]
    )
    lefts, rights = gather(left_rows, right_rows)
    left_keep, left_send, first_keep, first_send, second_keep, second_send = triples(
        jnp.stack([row, col]).astype(jnp.int32),
        lefts,
        rights,
        cotangent.reshape(-1, width),
        query_weight,
        key_weight,
        left_weight,
        right_weight,
        out_weight,
    )

    core = col & 1
    first_came = send(first_send, "row", 4)
    second_came = send(second_send, "row", 12)
    left_total = add_up(left_keep, [send(left_send, "col", 1)])
    low = left_total.astype(BF)
    came = [
        send(jnp.concatenate([low[256 * k : 256 * k + 256], low[1024:]]), "col", 4 * k).astype(F32)
        for k in (1, 2, 3)
    ]
    first_came, second_came, came[0] = lax.optimization_barrier((first_came, second_came, came[0]))
    kept = jnp.concatenate([left_total[:256], low[1024:].astype(F32)])
    total = (kept + came[0]) + (came[1] + came[2])
    low = total[128:].astype(BF)
    first = add_up(first_keep, [first_came])
    second = add_up(second_keep, [second_came])
    first_came = send(first[2:].astype(BF), "row", 12)
    second_came = send(second[2:].astype(BF), "row", 4)
    first_came, second_came, low = lax.optimization_barrier((first_came, second_came, low))
    came = send(low, "col", 2).astype(F32)
    left_grad = total[:128] + came[:128]
    weights = low[128:].astype(F32) + came[128:]
    right_total = jnp.concatenate(
        [add_up(first[:2], [first_came]), add_up(second[:2], [second_came])]
    )
    low = right_total.astype(BF)
    right_came = lax.all_to_all(low, "row", 0, 0, axis_index_groups=LINES)
    weights = meet(weights.astype(BF), "row", (4, 8, 12)).astype(BF)
    right_came, weights = lax.optimization_barrier((right_came, weights))
    weights = meet(weights, "row", (1, 2, 3))
    right_grad = jnp.sum(right_came.astype(F32), axis=0)
    right_grad = jnp.swapaxes(right_grad.reshape(16, 16, width), 0, 1)
    mine = weights.astype(BF)
    other = send(mine, "col", 1)
    first = jnp.where(core == 0, mine, other)
    second = jnp.where(core == 0, other, mine)
    weights = jnp.concatenate([first, second]).astype(F32)
    proj_grads = weights[:512].reshape(4, 128, width)
    return (left_grad.reshape(left_edges.shape), right_grad, proj_grads, weights[512:])


def solution(mesh):
    return jax.shard_map(
        body,
        mesh=mesh,
        in_specs=(
            P("row", "col", None),
            P("row", "col", None),
            P("row", "col"),
            P("row", "col"),
            P("row", "col", None),
            P(),
            P(),
            P(),
            P(),
            P(),
        ),
        out_specs=(P("row", "col", None), P("row", "col", None), P(), P()),
        check_vma=False,
    )
```

```python
import math

import jax
import jax.numpy as jnp
from jax import lax
from jax.experimental import pallas as pl
from jax.experimental.pallas import tpu as pltpu
from jax.sharding import PartitionSpec as P

HEADS = 4
HEAD_DIM = 32
BF = jnp.bfloat16
F32 = jnp.float32


LINES = [[4 * x + z for z in range(4)] for x in range(4)]


def flip(k):
    return [(i, i ^ k) for i in range(16)]


def send(block, axis, k):
    with jax.named_scope("s_" + axis + str(k)):
        return lax.ppermute(block, axis, flip(k))


def gather(left, right):
    came = [send(right, "row", k) for k in (1, 2, 3)]
    came[0], left = lax.optimization_barrier((came[0], left))
    line = jnp.stack([right] + came)
    near = send(line, "row", 4)
    far = send(line, "row", 12)
    pair = jnp.stack([left, send(left, "col", 2)])
    near, pair = lax.optimization_barrier((near, pair))
    first = send(far[:2], "row", 4)
    second = send(near[2:], "row", 12)
    quads = jnp.concatenate([pair] + [send(pair, "col", k) for k in (4, 8, 12)])
    first, second, quads = lax.optimization_barrier((first, second, quads))
    return (quads, send(quads, "col", 1)), (line, near, far, first, second)


def left_place(col, b):
    apart = col ^ b
    return (apart & 1) * 8 + (apart >> 2) * 2 + ((apart >> 1) & 1)


def add_up(own, others):
    total = own.astype(F32)
    for other in others:
        total = total + other.astype(F32)
    return total


def meet(own, axis, flips):
    came = [send(own, axis, k).astype(F32) for k in flips]
    return (own.astype(F32) + came[0]) + (came[1] + came[2])


def nt(a, b):
    return lax.dot_general(a, b, (((1,), (1,)), ((), ())), preferred_element_type=F32)


def nn(a, b):
    return jnp.dot(a, b, preferred_element_type=F32)


def tn(a, b):
    return lax.dot_general(a, b, (((0,), (0,)), ((), ())), preferred_element_type=F32)


def fold(tiles):
    place = lax.broadcasted_iota(jnp.int32, tiles[0].shape, 0)
    low = place < 4
    fours = [
        jnp.where(low, tiles[n], tiles[n + 4])
        + pltpu.roll(jnp.where(low, tiles[n + 4], tiles[n]), 4, 0)
        for n in range(4)
    ]
    low = (place & 2) == 0
    twos = [
        jnp.where(
            low,
            fours[n] + pltpu.roll(fours[n], 6, 0),
            fours[n + 2] + pltpu.roll(fours[n + 2], 2, 0),
        )
        for n in range(2)
    ]
    return jnp.where(
        (place & 1) == 0,
        twos[0] + pltpu.roll(twos[0], 7, 0),
        twos[1] + pltpu.roll(twos[1], 1, 0),
    )


def triple_kernel(
    at_ref,
    left0,
    left1,
    right0,
    right1,
    right3,
    right2a,
    right2b,
    cot_hbm,
    wq_hbm,
    wk_hbm,
    wl_hbm,
    wr_hbm,
    wo_hbm,
    lkeep,
    lsend,
    akeep,
    asend,
    bkeep,
    bsend,
    xl,
    xr,
    ql,
    kr,
    gql,
    gkr,
    ub,
    ts,
    tg,
    pb,
    sb,
    att,
    lb,
    rb,
    rp,
    vr,
    up,
    vb,
    wb,
    cot_ref,
    weights,
    arrived,
):
    scaling = 1.0 / math.sqrt(HEAD_DIM)
    copies = [
        pltpu.make_async_copy(ref, weights.at[n], arrived.at[n])
        for n, ref in enumerate((wq_hbm, wl_hbm, wk_hbm, wr_hbm, wo_hbm))
    ]
    copies.append(pltpu.make_async_copy(cot_hbm, cot_ref, arrived.at[5]))
    for copy in copies:
        copy.start()
    row = at_ref[0]
    col = at_ref[1]
    lefts = (left0, left1)
    rights = (
        [(right0, z) for z in range(4)]
        + [(right1, z) for z in range(4)]
        + [(right2a, 0), (right2a, 1), (right2b, 0), (right2b, 1)]
        + [(right3, z) for z in range(4)]
    )
    outs = [None] * 16
    for z in range(2):
        outs[z], outs[12 + z] = (akeep, z), (akeep, 2 + z)
        outs[4 + z], outs[8 + z] = (asend, z), (asend, 2 + z)
        outs[2 + z], outs[6 + z] = (bkeep, z), (bkeep, 2 + z)
        outs[14 + z], outs[10 + z] = (bsend, z), (bsend, 2 + z)
    slots = [left_place(col, row ^ t) for t in range(16)]

    lane = lax.broadcasted_iota(jnp.int32, (16, 128), 1) // 16
    half0 = jnp.zeros((16, 128), F32)
    half1 = jnp.zeros((16, 128), F32)
    for t in range(16):
        slot = slots[t]
        block, z = rights[t]
        for j in range(16):
            xr[j, slot] = block[z, 16 * j : 16 * j + 16, :]
        came = block[z, 256:272, :].astype(F32)
        half0 = jnp.where(lane == slot, came, half0)
        half1 = jnp.where(lane + 8 == slot, came, half1)
    right_allowed = jnp.concatenate([half0, half1], axis=1)
    spread4 = (
        lax.broadcasted_iota(jnp.int32, (64, 16), 0) // 4
        == lax.broadcasted_iota(jnp.int32, (64, 16), 1)
    ).astype(BF)
    right_allowed = nn(spread4, right_allowed.astype(BF))
    halves = []
    for half in range(2):
        total = jnp.zeros((16, 128), F32)
        for s in range(8):
            total = jnp.where(lane == s, lefts[half][s, 128:144, :].astype(F32), total)
        halves.append(total)
    left_allowed = jnp.concatenate(halves, axis=1)

    for i in range(8):
        for s in range(16):
            xl[i, s] = lefts[s // 8][s % 8, 16 * i : 16 * i + 16, :]
    for copy in copies:
        copy.wait()
    wl = jnp.concatenate([weights[0].T, weights[1].T])
    wr = jnp.concatenate([weights[2].T, weights[3].T])

    def project_left(i, _):
        both = nt(wl, xl[i].reshape(256, 128)).astype(BF)
        ql[i] = both.astype(F32)
        vb[i] = both[128:]
        return 0

    lax.fori_loop(0, 8, project_left, 0, unroll=8)

    def project_right(j, _):
        both = nt(wr, xr[j].reshape(256, 128)).astype(BF)
        kr[j] = both.astype(F32)
        wb[j] = both[128:]
        return 0

    lax.fori_loop(0, 16, project_right, 0, unroll=8)
    cot = cot_ref[...]
    pick = (
        lax.broadcasted_iota(jnp.int32, (16, 2048), 1) // 128
        == lax.broadcasted_iota(jnp.int32, (16, 2048), 0)
    ).astype(BF)
    wo = weights[4]

    up[...] = nt(cot, wo).astype(BF).astype(F32)
    place = lax.broadcasted_iota(jnp.int32, (8, 256), 0)
    heads = lax.broadcasted_iota(jnp.int32, (8, 256), 1) // 32
    agree = place == heads

    def grad_row(i):
        for jj in range(8):
            both = jnp.concatenate(
                [
                    jnp.broadcast_to(up[pl.ds(i * 16 + 2 * jj + n, 1), :], (8, 128))
                    for n in range(2)
                ],
                axis=1,
            )
            both = jnp.where(agree, both, 0.0).astype(BF)
            tg[i, pl.ds(8 * jj, 8), :] = nn(both, vr[i, jj])

    def score_row(i, _):
        mine = cot_ref[pl.ds(pl.multiple_of(i * 16, 16), 16), :]
        spread = nn(nt(wo, mine).astype(BF), pick)
        for j in range(16):
            ub[i * 16 + j] = spread[:, 128 * j : 128 * j + 128]
        grad_row(jnp.maximum(i - 1, 0))
        for h in range(4):
            tiles = [pl.ds(h * 32 + 8 * e, 8) for e in range(4)]
            q = [ql[i, r, :] for r in tiles]
            v = vb[i, pl.ds(h * 32, 32), :]
            for half in range(2):
                scores = []
                for j in range(8 * half, 8 * half + 8):
                    k = [kr[j, r, :] for r in tiles]
                    scores.append((q[0] * k[0] + q[1] * k[1]) + (q[2] * k[2] + q[3] * k[3]))
                    w = wb[j, pl.ds(h * 32, 32), :]
                    vr[i, j // 2, pl.ds(j % 2 * 128 + h * 32, 32), :] = v * w
                score = fold(scores)
                for side in range(2):
                    ts[i, side, pl.ds(32 * half + h, 8, stride=4), :] = score[
                        :, 128 * side : 128 * side + 128
                    ]
        return 0

    lax.fori_loop(0, 8, score_row, 0, unroll=4)
    grad_row(7)

    for i in range(8):
        for part in range(2):
            rows = pl.ds(32 * part, 32)
            allowed = right_allowed[32 * part : 32 * part + 32] * left_allowed[i : i + 1, :] > 0.5
            score = jnp.concatenate([ts[i, 0, rows, :], ts[i, 1, rows, :]], axis=1)
            score = jnp.where(allowed, score * scaling, -1000000000.0)
            grad = tg[i, rows, :]
            top = jnp.max(score, axis=1, keepdims=True)
            raw = jnp.exp(score - top)
            prob = raw / jnp.sum(raw, axis=1, keepdims=True)
            mean = jnp.sum(prob * grad, axis=1, keepdims=True)
            grad = prob * (grad - mean) * scaling
            pb[i, rows, :] = prob.astype(BF).astype(F32)
            sb[i, rows, :] = grad.astype(BF).astype(F32)

    def gradients(t, _):
        h = t // 4
        rows = pl.ds(pl.multiple_of(t * 8, 8), 8)
        lower = pl.ds(pl.multiple_of(128 + t * 8, 8), 8)
        seen = []
        for n in range(4):
            jj = t % 2 * 4 + n
            prob = pb[t // 2, pl.ds(pl.multiple_of(8 * jj, 8), 8), :].astype(BF)
            part = jnp.where(agree, nt(prob, vr[t // 2, jj]), 0.0)
            seen += [part[:, :128], part[:, 128:]]
        att[rows, :] = fold(seen)
        for ib in range(2):
            group = range(4 * ib, 4 * ib + 4)
            q = [ql[i, rows, :] for i in group]
            v = [ql[i, lower, :] for i in group]
            gq = [jnp.zeros((8, 256), F32) for _ in group]
            gl = [jnp.zeros((8, 256), F32) for _ in group]
            for j in range(16):
                k = kr[j, rows, :]
                w = kr[j, lower, :]
                at = pl.ds(j * 4 + h, 1)
                if ib == 0:
                    gk = jnp.zeros((8, 256), F32)
                    gr = jnp.zeros((8, 256), F32)
                else:
                    gk = gkr[j, rows, :]
                    gr = gkr[j, lower, :]
                for n, i in enumerate(group):
                    p = jnp.broadcast_to(pb[i, at, :], (8, 256))
                    s = jnp.broadcast_to(sb[i, at, :], (8, 256))
                    u = ub[i * 16 + j, rows, :]
                    pu = p * jnp.concatenate([u, u], axis=1)
                    gl[n] = gl[n] + pu * w
                    gr = gr + pu * v[n]
                    gq[n] = gq[n] + s * k
                    gk = gk + s * q[n]
                gkr[j, rows, :] = gk
                gkr[j, lower, :] = gr
            for n, i in enumerate(group):
                gql[i, rows, :] = gq[n]
                gql[i, lower, :] = gl[n]
        return 0

    lax.fori_loop(0, 16, gradients, 0, unroll=2)

    def finish(n, _):
        g = gql[n].astype(BF)
        lb[:, pl.ds(pl.multiple_of(n * 256, 256), 256)] = g
        part = tn(g, wl).astype(BF).reshape(16, 16, 128)
        for s in range(16):
            rows = pl.ds(pl.multiple_of(s % 8 * 128 + n * 16, 16), 16)
            (lkeep, lsend)[s // 8][rows, :] = part[s]
        for m in range(2):
            j = 2 * n + m
            g = gkr[j].astype(BF)
            rb[:, pl.ds(pl.multiple_of(j * 256, 256), 256)] = g
            rp[j] = tn(g, wr).astype(BF).reshape(16, 16, 128)
            rows = pl.ds(pl.multiple_of(j * 16, 16), 16)
            for t in range(16):
                out, z = outs[t]
                out[z, rows, :] = rp[j, left_place(col, row // 4 * 4 ^ t)]
        return 0

    lax.fori_loop(0, 8, finish, 0, unroll=8)
    lsum = nn(lb[...], xl[...].reshape(2048, 128))
    rsum = nn(rb[...], xr[...].reshape(4096, 128))
    sums = jnp.concatenate(
        [
            lsum[:128].T,
            rsum[:128].T,
            lsum[128:].T,
            rsum[128:].T,
            tn(att[...].astype(BF), cot),
        ]
    )
    even = (col & 1) == 0
    lkeep[1024:1344, :] = jnp.where(even, sums[:320], sums[320:]).astype(BF)
    lsend[1024:1344, :] = jnp.where(even, sums[320:], sums[:320]).astype(BF)


def triples(at, lefts, rights, cot, wq, wk, wl, wr, wo):
    vmem = pl.BlockSpec(memory_space=pltpu.VMEM)
    return pl.pallas_call(
        triple_kernel,
        out_shape=(
            jax.ShapeDtypeStruct((1344, 128), BF),
            jax.ShapeDtypeStruct((1344, 128), BF),
            jax.ShapeDtypeStruct((4, 256, 128), BF),
            jax.ShapeDtypeStruct((4, 256, 128), BF),
            jax.ShapeDtypeStruct((4, 256, 128), BF),
            jax.ShapeDtypeStruct((4, 256, 128), BF),
        ),
        in_specs=[pl.BlockSpec(memory_space=pltpu.SMEM)]
        + [vmem] * 7
        + [pl.BlockSpec(memory_space=pl.ANY)] * 6,
        out_specs=(vmem,) * 6,
        scratch_shapes=[
            pltpu.VMEM((8, 16, 16, 128), BF),
            pltpu.VMEM((16, 16, 16, 128), BF),
            pltpu.VMEM((8, 256, 256), F32),
            pltpu.VMEM((16, 256, 256), F32),
            pltpu.VMEM((8, 256, 256), F32),
            pltpu.VMEM((16, 256, 256), F32),
            pltpu.VMEM((128, 128, 128), F32),
            pltpu.VMEM((8, 2, 64, 128), F32),
            pltpu.VMEM((8, 64, 256), F32),
            pltpu.VMEM((8, 64, 256), F32),
            pltpu.VMEM((8, 64, 256), F32),
            pltpu.VMEM((128, 128), F32),
            pltpu.VMEM((256, 2048), BF),
            pltpu.VMEM((256, 4096), BF),
            pltpu.VMEM((16, 16, 16, 128), BF),
            pltpu.VMEM((8, 8, 256, 256), BF),
            pltpu.VMEM((128, 128), F32),
            pltpu.VMEM((8, 128, 256), BF),
            pltpu.VMEM((16, 128, 256), BF),
            pltpu.VMEM((128, 128), BF),
            pltpu.VMEM((5, 128, 128), BF),
            pltpu.SemaphoreType.DMA((6,)),
        ],
        compiler_params=pltpu.CompilerParams(vmem_limit_bytes=48 * 1024 * 1024),
        cost_estimate=pl.CostEstimate(
            flops=800_000_000, bytes_accessed=5_000_000, transcendentals=131072
        ),
    )(at, *lefts, *rights, cot, wq, wk, wl, wr, wo)


def body(
    left_edges,
    right_edges,
    left_mask,
    right_mask,
    cotangent,
    query_weight,
    key_weight,
    left_weight,
    right_weight,
    out_weight,
):
    width = left_edges.shape[2]
    row = lax.axis_index("row")
    col = lax.axis_index("col")
    left_rows = jnp.concatenate(
        [
            left_edges.reshape(-1, width),
            jnp.pad(jnp.tile(left_mask.astype(BF), (1, 8)), ((0, 8), (0, 0))),
        ]
    )
    right_rows = jnp.concatenate(
        [
            jnp.swapaxes(right_edges, 0, 1).reshape(-1, width),
            jnp.tile(right_mask.T.astype(BF), (1, 8)),
        ]
    )
    lefts, rights = gather(left_rows, right_rows)
    left_keep, left_send, first_keep, first_send, second_keep, second_send = triples(
        jnp.stack([row, col]).astype(jnp.int32),
        lefts,
        rights,
        cotangent.reshape(-1, width),
        query_weight,
        key_weight,
        left_weight,
        right_weight,
        out_weight,
    )

    core = col & 1
    first_came = send(first_send, "row", 4)
    second_came = send(second_send, "row", 12)
    left_total = add_up(left_keep, [send(left_send, "col", 1)])
    low = left_total.astype(BF)
    came = [
        send(jnp.concatenate([low[256 * k : 256 * k + 256], low[1024:]]), "col", 4 * k).astype(F32)
        for k in (1, 2, 3)
    ]
    first_came, second_came, came[0] = lax.optimization_barrier((first_came, second_came, came[0]))
    kept = jnp.concatenate([left_total[:256], low[1024:].astype(F32)])
    total = (kept + came[0]) + (came[1] + came[2])
    low = total[128:].astype(BF)
    first = add_up(first_keep, [first_came])
    second = add_up(second_keep, [second_came])
    first_came = send(first[2:].astype(BF), "row", 12)
    second_came = send(second[2:].astype(BF), "row", 4)
    first_came, second_came, low = lax.optimization_barrier((first_came, second_came, low))
    came = send(low, "col", 2).astype(F32)
    left_grad = total[:128] + came[:128]
    weights = low[128:].astype(F32) + came[128:]
    right_total = jnp.concatenate(
        [add_up(first[:2], [first_came]), add_up(second[:2], [second_came])]
    )
    low = right_total.astype(BF)
    right_came = lax.all_to_all(low, "row", 0, 0, axis_index_groups=LINES)
    weights = meet(weights.astype(BF), "row", (4, 8, 12)).astype(BF)
    right_came, weights = lax.optimization_barrier((right_came, weights))
    weights = meet(weights, "row", (1, 2, 3))
    right_grad = jnp.sum(right_came.astype(F32), axis=0)
    right_grad = jnp.swapaxes(right_grad.reshape(16, 16, width), 0, 1)
    mine = weights.astype(BF)
    other = send(mine, "col", 1)
    first = jnp.where(core == 0, mine, other)
    second = jnp.where(core == 0, other, mine)
    weights = jnp.concatenate([first, second]).astype(F32)
    proj_grads = weights[:512].reshape(4, 128, width)
    return (left_grad.reshape(left_edges.shape), right_grad, proj_grads, weights[512:])


def solution(mesh):
    return jax.shard_map(
        body,
        mesh=mesh,
        in_specs=(
            P("row", "col", None),
            P("row", "col", None),
            P("row", "col"),
            P("row", "col"),
            P("row", "col", None),
            P(),
            P(),
            P(),
            P(),
            P(),
        ),
        out_specs=(P("row", "col", None), P("row", "col", None), P(), P()),
        check_vma=False,
    )
```
